512 devices in a mesh: pipe: 16 (over z, core), head: 32 (over y, x).
Axes of the slice: x: 4, y: 8, z: 8, core: 2. Of those that a mesh axis runs over, the one named last changes fastest.
Arguments:
- query: bfloat16 [4096, 4096], P(('pipe', 'head')), may hold values from -12 to 12
- key: bfloat16 [4096, 4096], P(('pipe', 'head')), may hold values from -6 to 6
- value: bfloat16 [4096, 4096], P(('pipe', 'head')), may hold values from -24 to 24
- stale_key: bfloat16 [2, 4096, 4096], P(None, 'pipe', 'head'), may hold values from -6 to 6
- stale_value: bfloat16 [2, 4096, 4096], P(None, 'pipe', 'head'), may hold values from -24 to 24
- patch_lengths: int32 [4], replicated, may hold values from 1 to 1536, 4096 in all
- stale_step: int32 [4], replicated, may hold values from 0 to 1
Outputs:
- attended: bfloat16 [4096, 4096], P(('pipe', 'head'))
The draws below stay inside these ranges and needn't reach their ends.
All inputs are finite; a program needn't handle non-finite values.
Results may differ from the reference program's by a relative error of at most 0.0085.
Values may be sent and summed in bfloat16 or wider, within the bound.
No kernel may reach another device: no remote copies, remote signals or barrier semaphores. Data moves between devices by JAX's collectives and lax.ppermute only.
A program may use at most 64 MiB of HBM per device.

```python
import math
import jax
import jax.numpy as jnp
import numpy as np
from jax import lax

HD = 128
PATCHES = 4
VERSIONS = 2
HEADS = 32
SEQ = 4096


def draw_query(key, part):
    key = jax.random.fold_in(key, 1)
    base = jnp.clip(2.0 * jax.random.normal(key, (SEQ, HEADS * HD), jnp.float32), -12.0, 12.0)
    return base.astype(jnp.bfloat16)


def draw_key(key, part):
    key = jax.random.fold_in(key, 2)
    base = jnp.clip(jax.random.normal(key, (SEQ, HEADS * HD), jnp.float32), -6.0, 6.0)
    return base.astype(jnp.bfloat16)


def draw_stale_key(key, part):
    key = jax.random.fold_in(key, 3)
    base = jnp.clip(jax.random.normal(key, (VERSIONS, SEQ, HEADS * HD), jnp.float32), -6.0, 6.0)
    return base.astype(jnp.bfloat16)


def set_ends(values, rng, least, high):
    index_at = [jax.random.randint(jax.random.fold_in(rng, axis), (), 0, length) for axis, length in enumerate(values.shape)]
    main_axis = values.shape.index(max(values.shape))
    beside = index_at[:main_axis] + [(index_at[main_axis] + 1) % values.shape[main_axis]] + index_at[main_axis + 1:]
    return values.at[tuple(index_at)].set(least).at[tuple(beside)].set(high)


def block_levels(stream_key, shape, shards, least, largest):
    level, own = 1.0, jax.random.fold_in(stream_key, 6)
    for axis_at, blocks in shards:
        draws = jnp.exp(jax.random.uniform(jax.random.fold_in(own, axis_at), (blocks,), jnp.float32, least / len(shards), largest / len(shards)))
        level = level * jnp.repeat(draws, shape[axis_at] // blocks).reshape([-1 if axis == axis_at else 1 for axis in range(len(shape))])
    return level


def profile(number_of, total, reach, skew):
    loads = [(1 << 20) // math.isqrt(rank ** skew) + 1 for rank in range(2, number_of + 1)]
    spare, counts = total - reach - (number_of - 1), [1] * (number_of - 1)
    while spare > 0:
        free = [i for i in range(number_of - 1) if counts[i] < reach]
        whole, left = sum([loads[i] for i in free]), spare
        for i in free:
            addition = min(reach - counts[i], max(1, left * loads[i] // whole), spare)
            counts[i] = counts[i] + addition
            spare = spare - addition
    return np.array([reach] + counts)


def uneven_parts(rng, count, total, limit, slope):
    if count == 2:
        one = jax.random.randint(rng, (), max(1, total - limit), min(limit, total - 1) + 1)
        return jnp.stack([one, total - one])
    lengths = jnp.asarray(profile(count, total, limit, slope), jnp.int32)
    twos = (count - 1) // 2
    source_of, sink = lengths[1:1 + 2 * twos:2], lengths[2:2 + 2 * twos:2]
    room = jnp.minimum(source_of - 1, limit - sink)
    shifted = jax.random.randint(jax.random.fold_in(rng, 1), (twos,), 0, 1 << 20) % (room + 1)
    lengths = lengths.at[1:1 + 2 * twos:2].set(source_of - shifted).at[2:2 + 2 * twos:2].set(sink + shifted)
    return lengths[jax.random.permutation(jax.random.fold_in(rng, 2), count)]


def bell_draw(key, shape, spread, most, pieces=(), held_as=jnp.bfloat16):
    factor_of = block_levels(key, shape, pieces, -0.22, 0.18) if pieces else 1.0
    entries = jax.random.normal(key, shape, jnp.float32) * spread * factor_of
    return jnp.minimum(jnp.maximum(entries, -most), most).astype(held_as)


def setup_inputs(seed: int = 0) -> dict:
    seeds = jax.random.split(jax.random.key(seed), 8)
    return {
        "query": draw_query(jax.random.fold_in(seeds[7], 71), 0),
        "key": draw_key(jax.random.fold_in(seeds[7], 71), 0),
        "value": bell_draw(seeds[2], (SEQ, HEADS * HD), 4.0, 24.0, ((0, 512),)),
        "stale_key": draw_stale_key(jax.random.fold_in(seeds[7], 71), 0),
        "stale_value": bell_draw(seeds[4], (VERSIONS, SEQ, HEADS * HD), 4.0, 24.0, ((1, 16), (2, 32))),
        "patch_lengths": uneven_parts(seeds[5], PATCHES, SEQ, 3 * SEQ // 8, 2).astype(jnp.int32),
        "stale_step": set_ends(jax.random.randint(seeds[6], (PATCHES,), 0, VERSIONS), jax.random.fold_in(seeds[6], 1), 0, VERSIONS - 1).astype(jnp.int32),
    }


def patch_index(positions, patch_lengths):
    bounds = jnp.cumsum(patch_lengths).astype(jnp.int32)
    return lax.optimization_barrier(jnp.sum((positions[:, None] >= bounds[None, :]).astype(jnp.int32), axis=1)).astype(jnp.int32)

def version_index(key_patch, stale_step):
    slots = jnp.arange(PATCHES, dtype=jnp.int32)
    picked = jnp.where(key_patch[:, None] == slots[None, :], stale_step[None, :], 0)
    return lax.optimization_barrier(jnp.sum(picked, axis=1)).astype(jnp.int32)

def reference(query, key, value, stale_key, stale_value, patch_lengths, stale_step):
    positions = jnp.arange(SEQ, dtype=jnp.int32)
    token_patch = patch_index(positions, patch_lengths)
    version = version_index(token_patch, stale_step)
    older = (version == 1)[:, None]
    stale_k = jnp.where(older, stale_key[1], stale_key[0])
    stale_v = jnp.where(older, stale_value[1], stale_value[0])

    def by_head(array):
        return jnp.transpose(array.reshape(SEQ, HEADS, HD), (1, 0, 2))
    block = math.gcd(1024, SEQ)
    blocks = SEQ // block
    scale = 1.0 / math.sqrt(HD)

    def one_head(operands):
        head_q, head_k, head_v, head_sk, head_sv = operands

        def one_block(index):
            first = (index * block).astype(jnp.int32)
            queries = lax.dynamic_slice_in_dim(head_q, first, block, 0)
            query_patch = lax.dynamic_slice_in_dim(token_patch, first, block, 0)
            fresh = token_patch[None, :] <= query_patch[:, None]
            fresh_scores = jnp.dot(queries, head_k.T, preferred_element_type=jnp.float32) * scale
            stale_scores = jnp.dot(queries, head_sk.T, preferred_element_type=jnp.float32) * scale
            scores = jnp.where(fresh, fresh_scores, stale_scores)
            peak = lax.optimization_barrier(jnp.max(scores, axis=1))
            weights = jnp.exp(scores - peak[:, None])
            total = lax.optimization_barrier(jnp.sum(weights, axis=1))
            rounded = weights.astype(jnp.bfloat16)
            zeros = jnp.zeros_like(rounded)
            summed = jnp.dot(jnp.where(fresh, rounded, zeros), head_v, preferred_element_type=jnp.float32)
            summed = summed + jnp.dot(jnp.where(fresh, zeros, rounded), head_sv, preferred_element_type=jnp.float32)
            return (summed / total[:, None]).astype(jnp.bfloat16)
        outputs = lax.map(one_block, jnp.arange(blocks, dtype=jnp.int32))
        return outputs.reshape(SEQ, HD)
    result = lax.map(one_head, (by_head(query), by_head(key), by_head(value), by_head(stale_k), by_head(stale_v)))
    return jnp.transpose(result, (1, 0, 2)).reshape(SEQ, HEADS * HD)
```

```python
import functools
import math

import jax
import jax.numpy as jnp
from jax import lax
from jax.experimental import pallas as pl
from jax.experimental.pallas import tpu as pltpu
from jax.sharding import Mesh, PartitionSpec as P

width = 128
span = 256
patches = 4
log2_scale = math.log2(math.e) / math.sqrt(width)

quad, pair, core, head = "za", "zb", "core", ("y", "x")
pipe = (quad, pair, core)
everywhere = pipe + head

whole_vmem = pl.BlockSpec(memory_space=pltpu.VMEM)
whole_smem = pl.BlockSpec(memory_space=pltpu.SMEM)


def patch_ends(lengths):
    ends, last = [], 0
    for m in range(patches):
        last = last + lengths[m]
        ends.append(last)
    return ends


def pick_stale(lengths, steps, keys, values, out, *, first):
    ends = patch_ends(lengths)
    position = first() + lax.broadcasted_iota(jnp.int32, (span, width), 0)
    step = jnp.full((span, width), steps[0], jnp.int32)
    for m in range(1, patches):
        step = jnp.where(position >= ends[m - 1], steps[m], step)
    older = step == 1
    for at, cache in enumerate((keys, values)):
        older_rows, newer_rows = cache[1].astype(jnp.float32), cache[0].astype(jnp.float32)
        out[:, at * width : (at + 1) * width] = jnp.where(older, older_rows, newer_rows).astype(jnp.bfloat16)


def attend(lengths, queries, own, other, stale_own, stale_core, stale_pair, stale_both, out, *, place):
    za, zb, c = place()
    ends = patch_ends(lengths)
    chip = 2 * span
    lane = lax.broadcasted_iota(jnp.int32, (span, width), 1)

    own_first = za * 1024 + zb * chip
    other_first = za * 1024 + (1 - zb) * chip
    own_rows = pl.ds(pl.multiple_of(c * span, span), span)
    away_rows = pl.ds(pl.multiple_of((1 - c) * span, span), span)
    groups = (
        (own, own_rows, stale_own, own_first + c * span),
        (own, away_rows, stale_core, own_first + (1 - c) * span),
        (other, own_rows, stale_pair, other_first + c * span),
        (other, away_rows, stale_both, other_first + (1 - c) * span),
    )
    key_offset = lax.broadcasted_iota(jnp.int32, (span, span), 1)
    row_offset = lax.broadcasted_iota(jnp.int32, (span, 1), 0)

    for at in range(4):
        rows = pl.ds(at * span, span)
        q = queries[rows, :]
        position = at * 1024 + zb * chip + c * span + row_offset
        reach = jnp.full((span, 1), ends[patches - 1], jnp.int32)
        for m in range(patches - 2, -1, -1):
            reach = jnp.where(position < ends[m], ends[m], reach)
        scores, fresh_at = [], []
        for fresh, where_rows, stale, first in groups:
            fresh_scores = lax.dot_general(
                q, fresh[where_rows, width : 2 * width], (((1,), (1,)), ((), ())), preferred_element_type=jnp.float32
            )
            stale_scores = lax.dot_general(
                q, stale[:, :width], (((1,), (1,)), ((), ())), preferred_element_type=jnp.float32
            )
            is_fresh = key_offset < reach - first
            fresh_at.append(is_fresh)
            scores.append(jnp.where(is_fresh, fresh_scores, stale_scores))
        peak = functools.reduce(jnp.maximum, scores)
        peak = jnp.max(peak, axis=1, keepdims=True) * log2_scale
        peak = peak.astype(jnp.bfloat16).astype(jnp.float32)
        weights = [jnp.exp2(s * log2_scale - peak) for s in scores]
        total = jnp.sum(functools.reduce(jnp.add, weights), axis=1, keepdims=True)
        summed = jnp.zeros((span, width), jnp.float32)
        for w, is_fresh, (fresh, where_rows, stale, first) in zip(weights, fresh_at, groups):
            summed += jnp.dot(
                jnp.where(is_fresh, w, 0.0).astype(jnp.bfloat16),
                fresh[where_rows, 2 * width : 3 * width],
                preferred_element_type=jnp.float32,
            )
            summed += jnp.dot(
                jnp.where(is_fresh, 0.0, w).astype(jnp.bfloat16),
                stale[:, width:],
                preferred_element_type=jnp.float32,
            )
        high = total.astype(jnp.bfloat16).astype(jnp.float32)
        stats = jnp.where(lane == 0, peak, jnp.where(lane == 1, high, total - high))
        out[rows, :width] = (summed / total).astype(jnp.bfloat16)
        out[rows, width:] = stats.astype(jnp.bfloat16)


def combine(parts, out):
    heads = out.shape[1] // width
    blocks = parts[...].astype(jnp.float32).reshape(4, heads, 8, 2 * width)
    outputs = blocks[..., :width]
    peaks = blocks[..., width : width + 1]
    totals = blocks[..., width + 1 : width + 2] + blocks[..., width + 2 : width + 3]
    shares = totals * jnp.exp2(peaks - jnp.max(peaks, axis=0, keepdims=True))
    shares = shares / jnp.sum(shares, axis=0, keepdims=True)
    joined = jnp.sum(outputs * shares, axis=0)
    for h in range(heads):
        out[:, h * width : (h + 1) * width] = joined[h].astype(jnp.bfloat16)


def on_device(query, key, value, stale_key, stale_value, patch_lengths, stale_step):
    def place():
        return lax.axis_index(quad), lax.axis_index(pair), lax.axis_index(core)

    za, zb, c = place()
    spot = jnp.stack([za, zb, c]).astype(jnp.int32)

    def by_head(x):
        return jnp.transpose(x.reshape(8, 32, width), (1, 0, 2))

    with jax.named_scope("tokens_to_heads"):
        mine = jnp.concatenate([by_head(query), by_head(key), by_head(value)], axis=2)
        mine = jnp.broadcast_to(mine[None], (2, 32, 8, 3 * width)).reshape(64, 8, 3 * width)
        own = lax.all_to_all(mine, (core,) + head, split_axis=0, concat_axis=0, tiled=True)
        own = own.reshape(2 * span, 3 * width)

    def select(lengths, steps, spot_ref, keys, values, out):
        first = lambda: spot_ref[0] * 1024 + spot_ref[1] * 512 + spot_ref[2] * 256
        pick_stale(lengths, steps, keys, values, out, first=first)

    with jax.named_scope("stale"):
        stale_own = pl.pallas_call(
            select,
            out_shape=jax.ShapeDtypeStruct((span, 2 * width), jnp.bfloat16),
            in_specs=[whole_smem] * 3 + [whole_vmem] * 2,
            out_specs=whole_vmem,
            name="pick_stale",
        )(patch_lengths, stale_step, spot, stale_key, stale_value)
        stale_core = lax.ppermute(stale_own, core, [(0, 1), (1, 0)])
        stale_pair = lax.ppermute(stale_own, pair, [(0, 1), (1, 0)])
        stale_both = lax.ppermute(stale_own, (pair, core), [(i, 3 - i) for i in range(4)])

    with jax.named_scope("swap"):
        other = lax.ppermute(own, pair, [(0, 1), (1, 0)])

    with jax.named_scope("gather_queries"):
        local_q = lax.dynamic_slice(own, (c * span, 0), (span, width))
        queries = lax.all_gather(local_q, quad, axis=0, tiled=True)

    def attend_here(lengths, spot_ref, *refs):
        attend(lengths, *refs, place=lambda: (spot_ref[0], spot_ref[1], spot_ref[2]))

    with jax.named_scope("attend"):
        parts = pl.pallas_call(
            attend_here,
            out_shape=jax.ShapeDtypeStruct((4 * span, 2 * width), jnp.bfloat16),
            in_specs=[whole_smem] * 2 + [whole_vmem] * 7,
            out_specs=whole_vmem,
            compiler_params=pltpu.CompilerParams(vmem_limit_bytes=40 * 1024 * 1024),
            cost_estimate=pl.CostEstimate(flops=2 * 2 * 1024 * 2048 * 128, bytes_accessed=3 << 20, transcendentals=1 << 20),
            name="attend",
        )(patch_lengths, spot, queries, own, other, stale_own, stale_core, stale_pair, stale_both)

    with jax.named_scope("heads_to_tokens"):
        parts = lax.all_to_all(
            parts.reshape(128, 8, 2 * width), (quad,) + head, split_axis=0, concat_axis=0, tiled=True
        )
        return pl.pallas_call(
            combine,
            out_shape=jax.ShapeDtypeStruct((8, 32 * width), jnp.bfloat16),
            in_specs=[whole_vmem],
            out_specs=whole_vmem,
            name="combine",
        )(parts.reshape(1024, 2 * width))


def solution(mesh):
    fine = Mesh(mesh.devices.reshape(4, 2, 2, 8, 4), (quad, pair, core) + head)
    rows = P(everywhere, None)
    cache = P(None, pipe, head)
    return jax.shard_map(
        on_device,
        mesh=fine,
        in_specs=(rows, rows, rows, cache, cache, P(), P()),
        out_specs=rows,
        check_vma=False,
    )
```

```python
import functools
import math

import jax
import jax.numpy as jnp
from jax import lax
from jax.experimental import pallas as pl
from jax.experimental.pallas import tpu as pltpu
from jax.sharding import Mesh, PartitionSpec as P

width = 128
span = 256
patches = 4
log2_scale = math.log2(math.e) / math.sqrt(width)

quad, pair, core, head = "za", "zb", "core", ("y", "x")
pipe = (quad, pair, core)
everywhere = pipe + head

whole_vmem = pl.BlockSpec(memory_space=pltpu.VMEM)
whole_smem = pl.BlockSpec(memory_space=pltpu.SMEM)


def patch_ends(lengths):
    ends, last = [], 0
    for m in range(patches):
        last = last + lengths[m]
        ends.append(last)
    return ends


def pick_stale(lengths, steps, keys, values, out, *, first):
    ends = patch_ends(lengths)
    position = first + lax.broadcasted_iota(jnp.int32, (span, width), 0)
    step = jnp.full((span, width), steps[0], jnp.int32)
    for m in range(1, patches):
        step = jnp.where(position >= ends[m - 1], steps[m], step)
    older = step == 1
    for at, cache in enumerate((keys, values)):
        older_rows, newer_rows = cache[1].astype(jnp.float32), cache[0].astype(jnp.float32)
        out[:, at * width : (at + 1) * width] = jnp.where(older, older_rows, newer_rows).astype(jnp.bfloat16)


def attend(lengths, own, away, same_core, other_core, stale, out, *, place):
    za, zb, c = place()
    ends = patch_ends(lengths)
    lane = lax.broadcasted_iota(jnp.int32, (span, width), 1)
    key_offset = lax.broadcasted_iota(jnp.int32, (span, span), 1)
    row_offset = lax.broadcasted_iota(jnp.int32, (span, 1), 0)

    for queries, pair_at in ((own, zb), (away, 1 - zb)):
        q = queries[...]
        position = za * 1024 + pair_at * 512 + c * span + row_offset
        reach = jnp.full((span, 1), ends[patches - 1], jnp.int32)
        for m in range(patches - 2, -1, -1):
            reach = jnp.where(position < ends[m], ends[m], reach)
        scores, fresh_at, values = [], [], []
        for at in range(4):
            for fresh, core_at in ((same_core, c), (other_core, 1 - c)):
                first = pl.multiple_of(at * 1024 + zb * 512 + core_at * span, span)
                rows, stale_rows = pl.ds(at * span, span), pl.ds(first, span)
                fresh_scores = lax.dot_general(
                    q, fresh[rows, :width], (((1,), (1,)), ((), ())), preferred_element_type=jnp.float32
                )
                stale_scores = lax.dot_general(
                    q, stale[stale_rows, :width], (((1,), (1,)), ((), ())), preferred_element_type=jnp.float32
                )
                is_fresh = key_offset < reach - first
                fresh_at.append(is_fresh)
                scores.append(jnp.where(is_fresh, fresh_scores, stale_scores))
                values.append((fresh, rows, stale_rows))
        peak = functools.reduce(jnp.maximum, scores)
        peak = jnp.max(peak, axis=1, keepdims=True) * log2_scale
        peak = peak.astype(jnp.bfloat16).astype(jnp.float32)
        weights = [jnp.exp2(s * log2_scale - peak) for s in scores]
        total = jnp.sum(functools.reduce(jnp.add, weights), axis=1, keepdims=True)
        summed = jnp.zeros((span, width), jnp.float32)
        for w, is_fresh, (fresh, rows, stale_rows) in zip(weights, fresh_at, values):
            summed += jnp.dot(
                jnp.where(is_fresh, w, 0.0).astype(jnp.bfloat16), fresh[rows, width:], preferred_element_type=jnp.float32
            )
            summed += jnp.dot(
                jnp.where(is_fresh, 0.0, w).astype(jnp.bfloat16),
                stale[stale_rows, width:],
                preferred_element_type=jnp.float32,
            )
        high = total.astype(jnp.bfloat16).astype(jnp.float32)
        stats = jnp.where(lane == 0, peak, jnp.where(lane == 1, high, total - high))
        out_rows = pl.ds(pl.multiple_of(pair_at * span, span), span)
        out[out_rows, :width] = (summed / total).astype(jnp.bfloat16)
        out[out_rows, width:] = stats.astype(jnp.bfloat16)


def combine(parts, out):
    heads = out.shape[1] // width
    blocks = parts[...].astype(jnp.float32).reshape(2, heads, 8, 2 * width)
    outputs = blocks[..., :width]
    peaks = blocks[..., width : width + 1]
    totals = blocks[..., width + 1 : width + 2] + blocks[..., width + 2 : width + 3]
    shares = totals * jnp.exp2(peaks - jnp.max(peaks, axis=0, keepdims=True))
    shares = shares / jnp.sum(shares, axis=0, keepdims=True)
    joined = jnp.sum(outputs * shares, axis=0)
    for h in range(heads):
        out[:, h * width : (h + 1) * width] = joined[h].astype(jnp.bfloat16)


def on_device(query, key, value, stale_key, stale_value, patch_lengths, stale_step):
    def place():
        return lax.axis_index(quad), lax.axis_index(pair), lax.axis_index(core)

    def select(lengths, steps, keys, values, out):
        za, zb, c = place()
        pick_stale(lengths, steps, keys, values, out, first=za * 1024 + zb * 512 + c * span)

    with jax.named_scope("stale"):
        stale_own = pl.pallas_call(
            select,
            out_shape=jax.ShapeDtypeStruct((span, 2 * width), jnp.bfloat16),
            in_specs=[whole_smem] * 2 + [whole_vmem] * 2,
            out_specs=whole_vmem,
            name="pick_stale",
        )(patch_lengths, stale_step, stale_key, stale_value)
        stale = lax.all_gather(stale_own, pipe, axis=0, tiled=True)

    def by_head(x):
        return jnp.transpose(x.reshape(8, 32, width), (1, 0, 2))

    with jax.named_scope("tokens_to_heads"):
        mine = jnp.concatenate([by_head(query), by_head(key), by_head(value)], axis=2)
        mine = lax.all_to_all(mine, head, split_axis=0, concat_axis=0, tiled=True)
        mine = mine.reshape(span, 3 * width)
        own_q, own_kv = mine[:, :width], mine[:, width:]

    with jax.named_scope("swap_queries"):
        away_q = lax.ppermute(own_q, pair, [(0, 1), (1, 0)])

    with jax.named_scope("gather_keys"):
        same_core = lax.all_gather(own_kv, quad, axis=0, tiled=True)
        other_core = lax.ppermute(same_core, core, [(0, 1), (1, 0)])

    with jax.named_scope("attend"):
        parts = pl.pallas_call(
            functools.partial(attend, place=place),
            out_shape=jax.ShapeDtypeStruct((2 * span, 2 * width), jnp.bfloat16),
            in_specs=[whole_smem] + [whole_vmem] * 5,
            out_specs=whole_vmem,
            compiler_params=pltpu.CompilerParams(vmem_limit_bytes=40 * 1024 * 1024),
            cost_estimate=pl.CostEstimate(flops=2 * 2 * 512 * 4096 * 128, bytes_accessed=4 << 20, transcendentals=1 << 20),
            name="attend",
        )(patch_lengths, own_q, away_q, same_core, other_core, stale)

    with jax.named_scope("heads_to_tokens"):
        parts = lax.all_to_all(parts.reshape(64, 8, 2 * width), (pair,) + head, split_axis=0, concat_axis=0, tiled=True)
        return pl.pallas_call(
            combine,
            out_shape=jax.ShapeDtypeStruct((8, 32 * width), jnp.bfloat16),
            in_specs=[whole_vmem],
            out_specs=whole_vmem,
            name="combine",
        )(parts.reshape(512, 2 * width))


def solution(mesh):
    fine = Mesh(mesh.devices.reshape(4, 2, 2, 8, 4), (quad, pair, core) + head)
    rows = P(everywhere, None)
    cache = P(None, pipe, head)
    return jax.shard_map(
        on_device,
        mesh=fine,
        in_specs=(rows, rows, rows, cache, cache, P(), P()),
        out_specs=rows,
        check_vma=False,
    )
```

```python
import functools
import math

import jax
import jax.numpy as jnp
from jax import lax
from jax.experimental import pallas as pl
from jax.experimental.pallas import tpu as pltpu
from jax.sharding import Mesh, PartitionSpec as P

width = 128
span = 256
patches = 4
log2_scale = math.log2(math.e) / math.sqrt(width)

quad, pair, core, head = "za", "zb", "core", ("y", "x")
pipe = (quad, pair, core)
everywhere = pipe + head

whole_vmem = pl.BlockSpec(memory_space=pltpu.VMEM)
whole_smem = pl.BlockSpec(memory_space=pltpu.SMEM)


def patch_ends(lengths):
    ends, last = [], 0
    for m in range(patches):
        last = last + lengths[m]
        ends.append(last)
    return ends


def pick_stale(lengths, steps, keys, values, out, *, first):
    ends = patch_ends(lengths)
    position = first + lax.broadcasted_iota(jnp.int32, (span, width), 0)
    step = jnp.full((span, width), steps[0], jnp.int32)
    for m in range(1, patches):
        step = jnp.where(position >= ends[m - 1], steps[m], step)
    older = step == 1
    for at, cache in enumerate((keys, values)):
        older_rows, newer_rows = cache[1].astype(jnp.float32), cache[0].astype(jnp.float32)
        out[:, at * width : (at + 1) * width] = jnp.where(older, older_rows, newer_rows).astype(jnp.bfloat16)


def attend(lengths, own, away, same_core, other_core, stale_same, stale_other, out, *, place):
    za, zb, c = place()
    ends = patch_ends(lengths)
    lane = lax.broadcasted_iota(jnp.int32, (span, width), 1)
    key_offset = lax.broadcasted_iota(jnp.int32, (span, span), 1)
    row_offset = lax.broadcasted_iota(jnp.int32, (span, 1), 0)

    for queries, pair_at in ((own, zb), (away, 1 - zb)):
        q = queries[...]
        position = za * 1024 + pair_at * 512 + c * span + row_offset
        reach = jnp.full((span, 1), ends[patches - 1], jnp.int32)
        for m in range(patches - 2, -1, -1):
            reach = jnp.where(position < ends[m], ends[m], reach)
        scores, fresh_at, values = [], [], []
        for ahead in range(4):
            at = lax.rem(za + ahead, 4)
            rows = pl.ds(pl.multiple_of(at * span, span), span)
            stale_rows = pl.ds(ahead * span, span)
            for fresh, stale, core_at in ((same_core, stale_same, c), (other_core, stale_other, 1 - c)):
                first = at * 1024 + zb * 512 + core_at * span
                fresh_scores = lax.dot_general(
                    q, fresh[rows, :width], (((1,), (1,)), ((), ())), preferred_element_type=jnp.float32
                )
                stale_scores = lax.dot_general(
                    q, stale[stale_rows, :width], (((1,), (1,)), ((), ())), preferred_element_type=jnp.float32
                )
                is_fresh = key_offset < reach - first
                fresh_at.append(is_fresh)
                scores.append(jnp.where(is_fresh, fresh_scores, stale_scores))
                values.append((fresh, rows, stale, stale_rows))
        peak = functools.reduce(jnp.maximum, scores)
        peak = jnp.max(peak, axis=1, keepdims=True) * log2_scale
        peak = peak.astype(jnp.bfloat16).astype(jnp.float32)
        weights = [jnp.exp2(s * log2_scale - peak) for s in scores]
        total = jnp.sum(functools.reduce(jnp.add, weights), axis=1, keepdims=True)
        summed = jnp.zeros((span, width), jnp.float32)
        for w, is_fresh, (fresh, rows, stale, stale_rows) in zip(weights, fresh_at, values):
            summed += jnp.dot(
                jnp.where(is_fresh, w, 0.0).astype(jnp.bfloat16), fresh[rows, width:], preferred_element_type=jnp.float32
            )
            summed += jnp.dot(
                jnp.where(is_fresh, 0.0, w).astype(jnp.bfloat16),
                stale[stale_rows, width:],
                preferred_element_type=jnp.float32,
            )
        high = total.astype(jnp.bfloat16).astype(jnp.float32)
        stats = jnp.where(lane == 0, peak, jnp.where(lane == 1, high, total - high))
        out_rows = pl.ds(pl.multiple_of(pair_at * span, span), span)
        out[out_rows, :width] = (summed / total).astype(jnp.bfloat16)
        out[out_rows, width:] = stats.astype(jnp.bfloat16)


def combine(parts, out):
    heads = out.shape[1] // width
    blocks = parts[...].astype(jnp.float32).reshape(2, heads, 8, 2 * width)
    outputs = blocks[..., :width]
    peaks = blocks[..., width : width + 1]
    totals = blocks[..., width + 1 : width + 2] + blocks[..., width + 2 : width + 3]
    shares = totals * jnp.exp2(peaks - jnp.max(peaks, axis=0, keepdims=True))
    shares = shares / jnp.sum(shares, axis=0, keepdims=True)
    joined = jnp.sum(outputs * shares, axis=0)
    for h in range(heads):
        out[:, h * width : (h + 1) * width] = joined[h].astype(jnp.bfloat16)


def on_device(query, key, value, stale_key, stale_value, patch_lengths, stale_step):
    def place():
        return lax.axis_index(quad), lax.axis_index(pair), lax.axis_index(core)

    def select(lengths, steps, keys, values, out):
        za, zb, c = place()
        pick_stale(lengths, steps, keys, values, out, first=za * 1024 + zb * 512 + c * span)

    swap = [(0, 1), (1, 0)]

    def by_head(x):
        return jnp.transpose(x.reshape(8, 32, width), (1, 0, 2))

    with jax.named_scope("tokens_to_heads"):
        mine = jnp.concatenate([by_head(query), by_head(key), by_head(value)], axis=2)
        mine = lax.all_to_all(mine, head, split_axis=0, concat_axis=0, tiled=True)
        mine = mine.reshape(span, 3 * width)

    with jax.named_scope("stale"):
        stale_own = pl.pallas_call(
            select,
            out_shape=jax.ShapeDtypeStruct((span, 2 * width), jnp.bfloat16),
            in_specs=[whole_smem] * 2 + [whole_vmem] * 2,
            out_specs=whole_vmem,
            name="pick_stale",
        )(patch_lengths, stale_step, stale_key, stale_value)
        stale_ahead = [
            lax.ppermute(stale_own, quad, [(i, i - ahead) for i in range(ahead, 4)]) for ahead in (1, 2, 3)
        ]

    mine, *stale_ahead = lax.optimization_barrier((mine, *stale_ahead))
    own_q, own_kv = mine[:, :width], mine[:, width:]

    with jax.named_scope("stale"):
        stale_same = jnp.concatenate([stale_own, *stale_ahead], axis=0)
        stale_other = lax.ppermute(stale_same, core, swap)

    with jax.named_scope("swap_queries"):
        away_q = lax.ppermute(own_q, pair, swap)

    with jax.named_scope("gather_keys"):
        same_core = jnp.broadcast_to(own_kv[None], (4, span, 2 * width))
        same_core = lax.all_to_all(same_core, quad, split_axis=0, concat_axis=0, tiled=True)
        same_core, stale_other, away_q = lax.optimization_barrier((same_core, stale_other, away_q))
        same_core = same_core.reshape(4 * span, 2 * width)
        other_core = lax.ppermute(same_core, core, swap)

    with jax.named_scope("attend"):
        parts = pl.pallas_call(
            functools.partial(attend, place=place),
            out_shape=jax.ShapeDtypeStruct((2 * span, 2 * width), jnp.bfloat16),
            in_specs=[whole_smem] + [whole_vmem] * 6,
            out_specs=whole_vmem,
            compiler_params=pltpu.CompilerParams(vmem_limit_bytes=40 * 1024 * 1024),
            cost_estimate=pl.CostEstimate(flops=2 * 2 * 512 * 4096 * 128, bytes_accessed=4 << 20, transcendentals=1 << 20),
            name="attend",
        )(patch_lengths, own_q, away_q, same_core, other_core, stale_same, stale_other)

    with jax.named_scope("heads_to_tokens"):
        parts = lax.all_to_all(parts.reshape(64, 8, 2 * width), (pair,) + head, split_axis=0, concat_axis=0, tiled=True)
        return pl.pallas_call(
            combine,
            out_shape=jax.ShapeDtypeStruct((8, 32 * width), jnp.bfloat16),
            in_specs=[whole_vmem],
            out_specs=whole_vmem,
            name="combine",
        )(parts.reshape(512, 2 * width))


def solution(mesh):
    fine = Mesh(mesh.devices.reshape(4, 2, 2, 8, 4), (quad, pair, core) + head)
    rows = P(everywhere, None)
    cache = P(None, pipe, head)
    return jax.shard_map(
        on_device,
        mesh=fine,
        in_specs=(rows, rows, rows, cache, cache, P(), P()),
        out_specs=rows,
        check_vma=False,
    )
```

```python
import functools
import math

import jax
import jax.numpy as jnp
from jax import lax
from jax.experimental import pallas as pl
from jax.experimental.pallas import tpu as pltpu
from jax.sharding import Mesh, PartitionSpec as P

width = 128
span = 256
patches = 4
log2_scale = math.log2(math.e) / math.sqrt(width)

quad, pair, core, head = "za", "zb", "core", ("y", "x")
pipe = (quad, pair, core)
everywhere = pipe + head

whole_vmem = pl.BlockSpec(memory_space=pltpu.VMEM)
whole_smem = pl.BlockSpec(memory_space=pltpu.SMEM)


def patch_ends(lengths):
    ends, last = [], 0
    for m in range(patches):
        last = last + lengths[m]
        ends.append(last)
    return ends


def pick_stale(lengths, steps, keys, values, out, *, first):
    ends = patch_ends(lengths)
    position = first + lax.broadcasted_iota(jnp.int32, (span, width), 0)
    step = jnp.full((span, width), steps[0], jnp.int32)
    for m in range(1, patches):
        step = jnp.where(position >= ends[m - 1], steps[m], step)
    older = step == 1
    for at, cache in enumerate((keys, values)):
        older_rows, newer_rows = cache[1].astype(jnp.float32), cache[0].astype(jnp.float32)
        out[:, at * width : (at + 1) * width] = jnp.where(older, older_rows, newer_rows).astype(jnp.bfloat16)


def attend(lengths, queries, own, *refs, place):
    fresh_refs, stale_refs, out = refs[:3], refs[3:7], refs[7]
    za, zb, c = place()
    ends = patch_ends(lengths)
    lane = lax.broadcasted_iota(jnp.int32, (span, width), 1)
    key_offset = lax.broadcasted_iota(jnp.int32, (span, span), 1)
    row_offset = lax.broadcasted_iota(jnp.int32, (span, 1), 0)

    blocks = []
    for at, (pair_at, core_at) in enumerate(((zb, c), (zb, 1 - c), (1 - zb, c), (1 - zb, 1 - c))):
        if at == 0:
            keys, values = own[:, width : 2 * width], own[:, 2 * width :]
        else:
            keys, values = fresh_refs[at - 1][:, :width], fresh_refs[at - 1][:, width:]
        stale_keys, stale_values = stale_refs[at][:, :width], stale_refs[at][:, width:]
        blocks.append((keys, values, stale_keys, stale_values, za * 1024 + pair_at * 512 + core_at * span))

    for at in range(4):
        rows = pl.ds(at * span, span)
        q = queries[rows, :]
        position = at * 1024 + zb * 512 + c * span + row_offset
        reach = jnp.full((span, 1), ends[patches - 1], jnp.int32)
        for m in range(patches - 2, -1, -1):
            reach = jnp.where(position < ends[m], ends[m], reach)
        scores, fresh_at = [], []
        for keys, _, stale_keys, _, first in blocks:
            fresh_scores = lax.dot_general(q, keys, (((1,), (1,)), ((), ())), preferred_element_type=jnp.float32)
            stale_scores = lax.dot_general(q, stale_keys, (((1,), (1,)), ((), ())), preferred_element_type=jnp.float32)
            is_fresh = key_offset < reach - first
            fresh_at.append(is_fresh)
            scores.append(jnp.where(is_fresh, fresh_scores, stale_scores))
        peak = functools.reduce(jnp.maximum, scores)
        peak = jnp.max(peak, axis=1, keepdims=True) * log2_scale
        peak = peak.astype(jnp.bfloat16).astype(jnp.float32)
        weights = [jnp.exp2(s * log2_scale - peak) for s in scores]
        total = jnp.sum(functools.reduce(jnp.add, weights), axis=1, keepdims=True)
        summed = jnp.zeros((span, width), jnp.float32)
        for w, is_fresh, (_, values, _, stale_values, _) in zip(weights, fresh_at, blocks):
            summed += jnp.dot(
                jnp.where(is_fresh, w, 0.0).astype(jnp.bfloat16), values, preferred_element_type=jnp.float32
            )
            summed += jnp.dot(
                jnp.where(is_fresh, 0.0, w).astype(jnp.bfloat16), stale_values, preferred_element_type=jnp.float32
            )
        high = total.astype(jnp.bfloat16).astype(jnp.float32)
        stats = jnp.where(lane == 0, peak, jnp.where(lane == 1, high, total - high))
        out[rows, :width] = (summed / total).astype(jnp.bfloat16)
        out[rows, width:] = stats.astype(jnp.bfloat16)


def combine(parts, out):
    heads = out.shape[1] // width
    blocks = parts[...].astype(jnp.float32).reshape(4, heads, 8, 2 * width)
    outputs = blocks[..., :width]
    peaks = blocks[..., width : width + 1]
    totals = blocks[..., width + 1 : width + 2] + blocks[..., width + 2 : width + 3]
    shares = totals * jnp.exp2(peaks - jnp.max(peaks, axis=0, keepdims=True))
    shares = shares / jnp.sum(shares, axis=0, keepdims=True)
    joined = jnp.sum(outputs * shares, axis=0)
    for h in range(heads):
        out[:, h * width : (h + 1) * width] = joined[h].astype(jnp.bfloat16)


def on_device(query, key, value, stale_key, stale_value, patch_lengths, stale_step):
    def place():
        return lax.axis_index(quad), lax.axis_index(pair), lax.axis_index(core)

    def select(lengths, steps, keys, values, out):
        za, zb, c = place()
        pick_stale(lengths, steps, keys, values, out, first=za * 1024 + zb * 512 + c * span)

    swap = [(0, 1), (1, 0)]

    def from_neighbours(x):
        return (
            lax.ppermute(x, core, swap),
            lax.ppermute(x, pair, swap),
            lax.ppermute(x, (pair, core), [(i, 3 - i) for i in range(4)]),
        )

    def by_head(x):
        return jnp.transpose(x.reshape(8, 32, width), (1, 0, 2))

    with jax.named_scope("tokens_to_heads"):
        mine = jnp.concatenate([by_head(query), by_head(key), by_head(value)], axis=2)
        mine = lax.all_to_all(mine, head, split_axis=0, concat_axis=0, tiled=True)
        mine = mine.reshape(span, 3 * width)

    with jax.named_scope("stale"):
        stale_own = pl.pallas_call(
            select,
            out_shape=jax.ShapeDtypeStruct((span, 2 * width), jnp.bfloat16),
            in_specs=[whole_smem] * 2 + [whole_vmem] * 2,
            out_specs=whole_vmem,
            name="pick_stale",
        )(patch_lengths, stale_step, stale_key, stale_value)
        stale = from_neighbours(stale_own)

    mine, *stale = lax.optimization_barrier((mine, *stale))

    with jax.named_scope("gather_queries"):
        queries = jnp.broadcast_to(mine[None, :, :width], (4, span, width))
        queries = lax.all_to_all(queries, quad, split_axis=0, concat_axis=0, tiled=True)
        queries = queries.reshape(4 * span, width)

    with jax.named_scope("neighbour_keys"):
        fresh = from_neighbours(mine[:, width:])

    with jax.named_scope("attend"):
        parts = pl.pallas_call(
            functools.partial(attend, place=place),
            out_shape=jax.ShapeDtypeStruct((4 * span, 2 * width), jnp.bfloat16),
            in_specs=[whole_smem] + [whole_vmem] * 9,
            out_specs=whole_vmem,
            compiler_params=pltpu.CompilerParams(vmem_limit_bytes=40 * 1024 * 1024),
            cost_estimate=pl.CostEstimate(flops=2 * 2 * 512 * 4096 * 128, bytes_accessed=4 << 20, transcendentals=1 << 20),
            name="attend",
        )(patch_lengths, queries, mine, *fresh, stale_own, *stale)

    with jax.named_scope("heads_to_tokens"):
        parts = lax.all_to_all(parts.reshape(128, 8, 2 * width), (quad,) + head, split_axis=0, concat_axis=0, tiled=True)
        return pl.pallas_call(
            combine,
            out_shape=jax.ShapeDtypeStruct((8, 32 * width), jnp.bfloat16),
            in_specs=[whole_vmem],
            out_specs=whole_vmem,
            name="combine",
        )(parts.reshape(1024, 2 * width))


def solution(mesh):
    fine = Mesh(mesh.devices.reshape(4, 2, 2, 8, 4), (quad, pair, core) + head)
    rows = P(everywhere, None)
    cache = P(None, pipe, head)
    return jax.shard_map(
        on_device,
        mesh=fine,
        in_specs=(rows, rows, rows, cache, cache, P(), P()),
        out_specs=rows,
        check_vma=False,
    )
```

```python
import functools
import math

import jax
import jax.numpy as jnp
from jax import lax
from jax.experimental import pallas as pl
from jax.experimental.pallas import tpu as pltpu
from jax.sharding import Mesh, PartitionSpec as P

width = 128
span = 256
patches = 4
log2_scale = math.log2(math.e) / math.sqrt(width)

quad, pair, core, head = "za", "zb", "core", ("y", "x")
pipe = (quad, pair, core)
everywhere = pipe + head

whole_vmem = pl.BlockSpec(memory_space=pltpu.VMEM)
small_kernel = pltpu.CompilerParams(vmem_limit_bytes=8 << 20)
whole_smem = pl.BlockSpec(memory_space=pltpu.SMEM)


def patch_ends(lengths):
    ends, last = [], 0
    for m in range(patches):
        last = last + lengths[m]
        ends.append(last)
    return ends


def pick_stale(lengths, steps, keys, values, out, *, first):
    ends = patch_ends(lengths)
    position = first + lax.broadcasted_iota(jnp.int32, (span, width), 0)
    step = jnp.full((span, width), steps[0], jnp.int32)
    for m in range(1, patches):
        step = jnp.where(position >= ends[m - 1], steps[m], step)
    older = step == 1
    for at, cache in enumerate((keys, values)):
        older_rows, newer_rows = cache[1].astype(jnp.float32), cache[0].astype(jnp.float32)
        out[:, at * width : (at + 1) * width] = jnp.where(older, older_rows, newer_rows).astype(jnp.bfloat16)


def attend(lengths, queries, fresh, stale, out, *, place):
    za, zb, c = place()
    ends = patch_ends(lengths)
    lane = lax.broadcasted_iota(jnp.int32, (span, width), 1)
    key_offset = lax.broadcasted_iota(jnp.int32, (span, span), 1)
    row_offset = lax.broadcasted_iota(jnp.int32, (span, 1), 0)

    blocks = []
    for at in range(4):
        rows = pl.ds(at * span, span)
        blocks.append((fresh[rows, :width], fresh[rows, width:], stale[rows, :width], stale[rows, width:], za * 1024 + at * span))

    for at in range(4):
        rows = pl.ds(at * span, span)
        q = queries[rows, :]
        position = at * 1024 + zb * 512 + c * span + row_offset
        reach = jnp.full((span, 1), ends[patches - 1], jnp.int32)
        for m in range(patches - 2, -1, -1):
            reach = jnp.where(position < ends[m], ends[m], reach)
        scores, fresh_at = [], []
        for keys, _, stale_keys, _, first in blocks:
            fresh_scores = lax.dot_general(q, keys, (((1,), (1,)), ((), ())), preferred_element_type=jnp.float32)
            stale_scores = lax.dot_general(q, stale_keys, (((1,), (1,)), ((), ())), preferred_element_type=jnp.float32)
            is_fresh = key_offset < reach - first
            fresh_at.append(is_fresh)
            scores.append(jnp.where(is_fresh, fresh_scores, stale_scores))
        peak = functools.reduce(jnp.maximum, scores)
        peak = jnp.max(peak, axis=1, keepdims=True) * log2_scale
        peak = peak.astype(jnp.bfloat16).astype(jnp.float32)
        weights = [jnp.exp2(s * log2_scale - peak) for s in scores]
        total = jnp.sum(functools.reduce(jnp.add, weights), axis=1, keepdims=True)
        summed = jnp.zeros((span, width), jnp.float32)
        for w, is_fresh, (_, values, _, stale_values, _) in zip(weights, fresh_at, blocks):
            summed += jnp.dot(
                jnp.where(is_fresh, w, 0.0).astype(jnp.bfloat16), values, preferred_element_type=jnp.float32
            )
            summed += jnp.dot(
                jnp.where(is_fresh, 0.0, w).astype(jnp.bfloat16), stale_values, preferred_element_type=jnp.float32
            )
        high = total.astype(jnp.bfloat16).astype(jnp.float32)
        stats = jnp.where(lane == 0, peak, jnp.where(lane == 1, high, total - high))
        out[rows, :width] = (summed / total).astype(jnp.bfloat16)
        out[rows, width:] = stats.astype(jnp.bfloat16)


def combine(parts, out):
    heads = out.shape[1] // width
    blocks = parts[...].astype(jnp.float32).reshape(4, heads, 8, 2 * width)
    outputs = blocks[..., :width]
    peaks = blocks[..., width : width + 1]
    totals = blocks[..., width + 1 : width + 2] + blocks[..., width + 2 : width + 3]
    shares = totals * jnp.exp2(peaks - jnp.max(peaks, axis=0, keepdims=True))
    shares = shares / jnp.sum(shares, axis=0, keepdims=True)
    joined = jnp.sum(outputs * shares, axis=0)
    for h in range(heads):
        out[:, h * width : (h + 1) * width] = joined[h].astype(jnp.bfloat16)


def on_device(query, key, value, stale_key, stale_value, patch_lengths, stale_step):
    def place():
        return lax.axis_index(quad), lax.axis_index(pair), lax.axis_index(core)

    def select(lengths, steps, keys, values, out):
        za, zb, c = place()
        pick_stale(lengths, steps, keys, values, out, first=za * 1024 + zb * 512 + c * span)

    swap = [(0, 1), (1, 0)]

    def from_neighbours(x):
        return lax.all_gather(x, (pair, core), axis=0, tiled=True)

    def by_head(x):
        return jnp.transpose(x.reshape(8, 32, width), (1, 0, 2))

    with jax.named_scope("tokens_to_heads"):
        mine = jnp.concatenate([by_head(query), by_head(key), by_head(value)], axis=2)
        mine = lax.all_to_all(mine, head, split_axis=0, concat_axis=0, tiled=True)
        mine = mine.reshape(span, 3 * width)

    with jax.named_scope("stale"):
        stale_own = pl.pallas_call(
            select,
            out_shape=jax.ShapeDtypeStruct((span, 2 * width), jnp.bfloat16),
            in_specs=[whole_smem] * 2 + [whole_vmem] * 2,
            out_specs=whole_vmem,
            compiler_params=small_kernel,
            name="pick_stale",
        )(patch_lengths, stale_step, stale_key, stale_value)
        stale = from_neighbours(stale_own)

    mine, stale = lax.optimization_barrier((mine, stale))

    with jax.named_scope("gather_queries"):
        queries = jnp.broadcast_to(mine[None, :, :width], (4, span, width))
        queries = lax.all_to_all(queries, quad, split_axis=0, concat_axis=0, tiled=True)
        queries = queries.reshape(4 * span, width)

    with jax.named_scope("neighbour_keys"):
        fresh = from_neighbours(mine[:, width:])

    with jax.named_scope("attend"):
        parts = pl.pallas_call(
            functools.partial(attend, place=place),
            out_shape=jax.ShapeDtypeStruct((4 * span, 2 * width), jnp.bfloat16),
            in_specs=[whole_smem] + [whole_vmem] * 3,
            out_specs=whole_vmem,
            compiler_params=pltpu.CompilerParams(vmem_limit_bytes=24 << 20),
            cost_estimate=pl.CostEstimate(flops=2 * 2 * 512 * 4096 * 128, bytes_accessed=4 << 20, transcendentals=1 << 20),
            name="attend",
        )(patch_lengths, queries, fresh, stale)

    with jax.named_scope("heads_to_tokens"):
        parts = lax.all_to_all(parts.reshape(128, 8, 2 * width), (quad,) + head, split_axis=0, concat_axis=0, tiled=True)
        return pl.pallas_call(
            combine,
            out_shape=jax.ShapeDtypeStruct((8, 32 * width), jnp.bfloat16),
            in_specs=[whole_vmem],
            out_specs=whole_vmem,
            compiler_params=small_kernel,
            name="combine",
        )(parts.reshape(1024, 2 * width))


def solution(mesh):
    fine = Mesh(mesh.devices.reshape(4, 2, 2, 8, 4), (quad, pair, core) + head)
    rows = P(everywhere, None)
    cache = P(None, pipe, head)
    return jax.shard_map(
        on_device,
        mesh=fine,
        in_specs=(rows, rows, rows, cache, cache, P(), P()),
        out_specs=rows,
        check_vma=False,
    )
```

```python
import functools
import math

import jax
import jax.numpy as jnp
from jax import lax
from jax.experimental import pallas as pl
from jax.experimental.pallas import tpu as pltpu
from jax.sharding import Mesh, PartitionSpec as P

width = 128
span = 256
patches = 4
log2_scale = math.log2(math.e) / math.sqrt(width)

quad, pair, core, head = "za", "zb", "core", ("y", "x")
pipe = (quad, pair, core)
everywhere = pipe + head

whole_vmem = pl.BlockSpec(memory_space=pltpu.VMEM)
small_kernel = pltpu.CompilerParams(vmem_limit_bytes=8 << 20)
whole_smem = pl.BlockSpec(memory_space=pltpu.SMEM)


def patch_ends(lengths):
    ends, last = [], 0
    for m in range(patches):
        last = last + lengths[m]
        ends.append(last)
    return ends


def pick_stale(lengths, steps, keys, values, out, *, first):
    ends = patch_ends(lengths)
    position = first + lax.broadcasted_iota(jnp.int32, (span, width), 0)
    step = jnp.full((span, width), steps[0], jnp.int32)
    for m in range(1, patches):
        step = jnp.where(position >= ends[m - 1], steps[m], step)
    older = step == 1
    for at, cache in enumerate((keys, values)):
        older_rows, newer_rows = cache[1].astype(jnp.float32), cache[0].astype(jnp.float32)
        out[:, at * width : (at + 1) * width] = jnp.where(older, older_rows, newer_rows).astype(jnp.bfloat16)


def attend(lengths, queries, fresh, stale, out, *, place):
    za, zb, c = place()
    ends = patch_ends(lengths)
    lane = lax.broadcasted_iota(jnp.int32, (span, width), 1)
    key_offset = lax.broadcasted_iota(jnp.int32, (span, span), 1)
    row_offset = lax.broadcasted_iota(jnp.int32, (span, 1), 0)

    blocks = []
    for at in range(4):
        rows = pl.ds(at * span, span)
        blocks.append((fresh[rows, :width], fresh[rows, width:], stale[rows, :width], stale[rows, width:], za * 1024 + at * span))

    for at in range(4):
        rows = pl.ds(at * span, span)
        q = queries[rows, :]
        position = at * 1024 + zb * 512 + c * span + row_offset
        reach = jnp.full((span, 1), ends[patches - 1], jnp.int32)
        for m in range(patches - 2, -1, -1):
            reach = jnp.where(position < ends[m], ends[m], reach)
        scores, fresh_at = [], []
        for keys, _, stale_keys, _, first in blocks:
            fresh_scores = lax.dot_general(q, keys, (((1,), (1,)), ((), ())), preferred_element_type=jnp.float32)
            stale_scores = lax.dot_general(q, stale_keys, (((1,), (1,)), ((), ())), preferred_element_type=jnp.float32)
            is_fresh = key_offset < reach - first
            fresh_at.append(is_fresh)
            scores.append(jnp.where(is_fresh, fresh_scores, stale_scores))
        peak = functools.reduce(jnp.maximum, scores)
        peak = jnp.max(peak, axis=1, keepdims=True) * log2_scale
        peak = peak.astype(jnp.bfloat16).astype(jnp.float32)
        weights = [jnp.exp2(s * log2_scale - peak) for s in scores]
        total = jnp.sum(functools.reduce(jnp.add, weights), axis=1, keepdims=True)
        summed = jnp.zeros((span, width), jnp.float32)
        for w, is_fresh, (_, values, _, stale_values, _) in zip(weights, fresh_at, blocks):
            summed += jnp.dot(
                jnp.where(is_fresh, w, 0.0).astype(jnp.bfloat16), values, preferred_element_type=jnp.float32
            )
            summed += jnp.dot(
                jnp.where(is_fresh, 0.0, w).astype(jnp.bfloat16), stale_values, preferred_element_type=jnp.float32
            )
        high = total.astype(jnp.bfloat16).astype(jnp.float32)
        stats = jnp.where(lane == 0, peak, jnp.where(lane == 1, high, total - high))
        out[rows, :width] = (summed / total).astype(jnp.bfloat16)
        out[rows, width:] = stats.astype(jnp.bfloat16)


def combine(parts, out):
    blocks = [parts[pl.ds(s * span, span), :].astype(jnp.float32) for s in range(4)]
    peaks = [b[:, width : width + 1] for b in blocks]
    totals = [b[:, width + 1 : width + 2] + b[:, width + 2 : width + 3] for b in blocks]
    top = functools.reduce(jnp.maximum, peaks)
    shares = [t * jnp.exp2(p - top) for t, p in zip(totals, peaks)]
    whole = functools.reduce(jnp.add, shares)
    joined = functools.reduce(jnp.add, [b[:, :width] * s for b, s in zip(blocks, shares)])
    out[...] = (joined / whole).astype(jnp.bfloat16)


def on_device(query, key, value, stale_key, stale_value, patch_lengths, stale_step):
    def place():
        return lax.axis_index(quad), lax.axis_index(pair), lax.axis_index(core)

    def select(lengths, steps, keys, values, out):
        za, zb, c = place()
        pick_stale(lengths, steps, keys, values, out, first=za * 1024 + zb * 512 + c * span)

    swap = [(0, 1), (1, 0)]

    def from_neighbours(x):
        return lax.all_gather(x, (pair, core), axis=0, tiled=True)

    def by_head(x):
        return jnp.transpose(x.reshape(8, 32, width), (1, 0, 2))

    with jax.named_scope("tokens_to_heads"):
        mine = jnp.concatenate([by_head(query), by_head(key), by_head(value)], axis=2)
        mine = lax.all_to_all(mine, head, split_axis=0, concat_axis=0, tiled=True)
        mine = mine.reshape(span, 3 * width)

    with jax.named_scope("stale"):
        stale_own = pl.pallas_call(
            select,
            out_shape=jax.ShapeDtypeStruct((span, 2 * width), jnp.bfloat16),
            in_specs=[whole_smem] * 2 + [whole_vmem] * 2,
            out_specs=whole_vmem,
            compiler_params=small_kernel,
            name="pick_stale",
        )(patch_lengths, stale_step, stale_key, stale_value)
        stale = from_neighbours(stale_own)

    mine, stale = lax.optimization_barrier((mine, stale))

    with jax.named_scope("gather_queries"):
        queries = jnp.broadcast_to(mine[None, :, :width], (4, span, width))
        queries = lax.all_to_all(queries, quad, split_axis=0, concat_axis=0, tiled=True)
        queries = queries.reshape(4 * span, width)

    with jax.named_scope("neighbour_keys"):
        fresh = from_neighbours(mine[:, width:])

    with jax.named_scope("attend"):
        parts = pl.pallas_call(
            functools.partial(attend, place=place),
            out_shape=jax.ShapeDtypeStruct((4 * span, 2 * width), jnp.bfloat16),
            in_specs=[whole_smem] + [whole_vmem] * 3,
            out_specs=whole_vmem,
            compiler_params=pltpu.CompilerParams(vmem_limit_bytes=24 << 20),
            cost_estimate=pl.CostEstimate(flops=2 * 2 * 512 * 4096 * 128, bytes_accessed=4 << 20, transcendentals=1 << 20),
            name="attend",
        )(patch_lengths, queries, fresh, stale)

    with jax.named_scope("join_partials"):
        parts = lax.all_to_all(parts.reshape(4, span, 2 * width), quad, split_axis=0, concat_axis=0, tiled=True)
        joined = pl.pallas_call(
            combine,
            out_shape=jax.ShapeDtypeStruct((span, width), jnp.bfloat16),
            in_specs=[whole_vmem],
            out_specs=whole_vmem,
            compiler_params=small_kernel,
            name="combine",
        )(parts.reshape(4 * span, 2 * width))

    with jax.named_scope("heads_to_tokens"):
        joined = lax.all_to_all(joined.reshape(32, 8, width), head, split_axis=0, concat_axis=0, tiled=True)
        return jnp.transpose(joined, (1, 0, 2)).reshape(8, 32 * width)


def solution(mesh):
    fine = Mesh(mesh.devices.reshape(4, 2, 2, 8, 4), (quad, pair, core) + head)
    rows = P(everywhere, None)
    cache = P(None, pipe, head)
    return jax.shard_map(
        on_device,
        mesh=fine,
        in_specs=(rows, rows, rows, cache, cache, P(), P()),
        out_specs=rows,
        check_vma=False,
    )
```

```python
import functools
import math

import jax
import jax.numpy as jnp
from jax import lax
from jax.experimental import pallas as pl
from jax.experimental.pallas import tpu as pltpu
from jax.sharding import Mesh, PartitionSpec as P

width = 128
span = 256
patches = 4
log2_scale = math.log2(math.e) / math.sqrt(width)

quad, pair, core, head = "za", "zb", "core", ("y", "x")
pipe = (quad, pair, core)
everywhere = pipe + head

whole_vmem = pl.BlockSpec(memory_space=pltpu.VMEM)
small_kernel = pltpu.CompilerParams(vmem_limit_bytes=8 << 20)
whole_smem = pl.BlockSpec(memory_space=pltpu.SMEM)


def patch_ends(lengths):
    ends, last = [], 0
    for m in range(patches):
        last = last + lengths[m]
        ends.append(last)
    return ends


def pick_stale(lengths, steps, keys, values, out, *, first):
    ends = patch_ends(lengths)
    position = first + lax.broadcasted_iota(jnp.int32, (span, width), 0)
    step = jnp.full((span, width), steps[0], jnp.int32)
    for m in range(1, patches):
        step = jnp.where(position >= ends[m - 1], steps[m], step)
    older = step == 1
    for at, cache in enumerate((keys, values)):
        older_rows, newer_rows = cache[1].astype(jnp.float32), cache[0].astype(jnp.float32)
        out[:, at * width : (at + 1) * width] = jnp.where(older, older_rows, newer_rows).astype(jnp.bfloat16)


def attend(lengths, own, away, fresh_same, fresh_other, stale_same, stale_other, out, *, place):
    za, zb, c = place()
    ends = patch_ends(lengths)
    lane = lax.broadcasted_iota(jnp.int32, (span, width), 1)
    key_offset = lax.broadcasted_iota(jnp.int32, (span, span), 1)
    row_offset = lax.broadcasted_iota(jnp.int32, (span, 1), 0)

    blocks = []
    for at in range(4):
        rows = pl.ds(at * span, span)
        for fresh, stale, core_at in ((fresh_same, stale_same, c), (fresh_other, stale_other, 1 - c)):
            first = at * 1024 + zb * 512 + core_at * span
            blocks.append((fresh[rows, :width], fresh[rows, width:], stale[rows, :width], stale[rows, width:], first))

    for queries, pair_at in ((own, zb), (away, 1 - zb)):
        q = queries[:, :width]
        position = za * 1024 + pair_at * 512 + c * span + row_offset
        reach = jnp.full((span, 1), ends[patches - 1], jnp.int32)
        for m in range(patches - 2, -1, -1):
            reach = jnp.where(position < ends[m], ends[m], reach)
        scores, fresh_at = [], []
        for keys, _, stale_keys, _, first in blocks:
            fresh_scores = lax.dot_general(q, keys, (((1,), (1,)), ((), ())), preferred_element_type=jnp.float32)
            stale_scores = lax.dot_general(q, stale_keys, (((1,), (1,)), ((), ())), preferred_element_type=jnp.float32)
            is_fresh = key_offset < reach - first
            fresh_at.append(is_fresh)
            scores.append(jnp.where(is_fresh, fresh_scores, stale_scores))
        peak = functools.reduce(jnp.maximum, scores)
        peak = jnp.max(peak, axis=1, keepdims=True) * log2_scale
        peak = peak.astype(jnp.bfloat16).astype(jnp.float32)
        weights = [jnp.exp2(s * log2_scale - peak) for s in scores]
        total = jnp.sum(functools.reduce(jnp.add, weights), axis=1, keepdims=True)
        summed = jnp.zeros((span, width), jnp.float32)
        for w, is_fresh, (_, values, _, stale_values, _) in zip(weights, fresh_at, blocks):
            summed += jnp.dot(
                jnp.where(is_fresh, w, 0.0).astype(jnp.bfloat16), values, preferred_element_type=jnp.float32
            )
            summed += jnp.dot(
                jnp.where(is_fresh, 0.0, w).astype(jnp.bfloat16), stale_values, preferred_element_type=jnp.float32
            )
        high = total.astype(jnp.bfloat16).astype(jnp.float32)
        stats = jnp.where(lane == 0, peak, jnp.where(lane == 1, high, total - high))
        rows = pl.ds(pl.multiple_of(pair_at * span, span), span)
        out[rows, :width] = (summed / total).astype(jnp.bfloat16)
        out[rows, width:] = stats.astype(jnp.bfloat16)


def combine(parts, out):
    heads = out.shape[1] // width
    blocks = parts[...].astype(jnp.float32).reshape(2, heads, 8, 2 * width)
    outputs = blocks[..., :width]
    peaks = blocks[..., width : width + 1]
    totals = blocks[..., width + 1 : width + 2] + blocks[..., width + 2 : width + 3]
    shares = totals * jnp.exp2(peaks - jnp.max(peaks, axis=0, keepdims=True))
    shares = shares / jnp.sum(shares, axis=0, keepdims=True)
    joined = jnp.sum(outputs * shares, axis=0)
    for h in range(heads):
        out[:, h * width : (h + 1) * width] = joined[h].astype(jnp.bfloat16)


def on_device(query, key, value, stale_key, stale_value, patch_lengths, stale_step):
    def place():
        return lax.axis_index(quad), lax.axis_index(pair), lax.axis_index(core)

    def select(lengths, steps, keys, values, out):
        za, zb, c = place()
        pick_stale(lengths, steps, keys, values, out, first=za * 1024 + zb * 512 + c * span)

    swap = [(0, 1), (1, 0)]

    def by_head(x):
        return jnp.transpose(x.reshape(8, 32, width), (1, 0, 2))

    with jax.named_scope("tokens_to_heads"):
        mine = jnp.concatenate([by_head(query), by_head(key), by_head(value)], axis=2)
        mine = lax.all_to_all(mine, head, split_axis=0, concat_axis=0, tiled=True)
        mine = mine.reshape(span, 3 * width)

    with jax.named_scope("stale"):
        stale_own = pl.pallas_call(
            select,
            out_shape=jax.ShapeDtypeStruct((span, 2 * width), jnp.bfloat16),
            in_specs=[whole_smem] * 2 + [whole_vmem] * 2,
            out_specs=whole_vmem,
            compiler_params=small_kernel,
            name="pick_stale",
        )(patch_lengths, stale_step, stale_key, stale_value)
        stale_same = lax.all_gather(stale_own, quad, axis=0, tiled=True)

    mine, stale_same = lax.optimization_barrier((mine, stale_same))

    with jax.named_scope("other_core_stale"):
        stale_other = lax.ppermute(stale_same, core, swap)

    with jax.named_scope("swap_queries"):
        away_q = lax.ppermute(mine[:, :width], pair, swap)

    with jax.named_scope("gather_keys"):
        fresh_same = jnp.broadcast_to(mine[None, :, width:], (4, span, 2 * width))
        fresh_same = lax.all_to_all(fresh_same, quad, split_axis=0, concat_axis=0, tiled=True)
        fresh_same, stale_other, away_q = lax.optimization_barrier((fresh_same, stale_other, away_q))
        fresh_same = fresh_same.reshape(4 * span, 2 * width)
        fresh_other = lax.ppermute(fresh_same, core, swap)

    with jax.named_scope("attend"):
        parts = pl.pallas_call(
            functools.partial(attend, place=place),
            out_shape=jax.ShapeDtypeStruct((2 * span, 2 * width), jnp.bfloat16),
            in_specs=[whole_smem] + [whole_vmem] * 6,
            out_specs=whole_vmem,
            compiler_params=pltpu.CompilerParams(vmem_limit_bytes=24 << 20),
            cost_estimate=pl.CostEstimate(flops=2 * 2 * 512 * 4096 * 128, bytes_accessed=4 << 20, transcendentals=1 << 20),
            name="attend",
        )(patch_lengths, mine, away_q, fresh_same, fresh_other, stale_same, stale_other)

    with jax.named_scope("heads_to_tokens"):
        parts = lax.all_to_all(parts.reshape(64, 8, 2 * width), (pair,) + head, split_axis=0, concat_axis=0, tiled=True)
        return pl.pallas_call(
            combine,
            out_shape=jax.ShapeDtypeStruct((8, 32 * width), jnp.bfloat16),
            in_specs=[whole_vmem],
            out_specs=whole_vmem,
            compiler_params=small_kernel,
            name="combine",
        )(parts.reshape(512, 2 * width))


def solution(mesh):
    fine = Mesh(mesh.devices.reshape(4, 2, 2, 8, 4), (quad, pair, core) + head)
    rows = P(everywhere, None)
    cache = P(None, pipe, head)
    return jax.shard_map(
        on_device,
        mesh=fine,
        in_specs=(rows, rows, rows, cache, cache, P(), P()),
        out_specs=rows,
        check_vma=False,
    )
```

```python
import functools
import math

import jax
import jax.numpy as jnp
from jax import lax
from jax.experimental import pallas as pl
from jax.experimental.pallas import tpu as pltpu
from jax.sharding import Mesh, PartitionSpec as P

width = 128
span = 256
patches = 4
log2_scale = math.log2(math.e) / math.sqrt(width)

quad, pair, core, head = "za", "zb", "core", ("y", "x")
pipe = (quad, pair, core)
everywhere = pipe + head

whole_vmem = pl.BlockSpec(memory_space=pltpu.VMEM)
small_kernel = pltpu.CompilerParams(vmem_limit_bytes=8 << 20)
whole_smem = pl.BlockSpec(memory_space=pltpu.SMEM)


def patch_ends(lengths):
    ends, last = [], 0
    for m in range(patches):
        last = last + lengths[m]
        ends.append(last)
    return ends


def pick_stale(lengths, steps, keys, values, out, *, first):
    ends = patch_ends(lengths)
    position = first + lax.broadcasted_iota(jnp.int32, (span, width), 0)
    step = jnp.full((span, width), steps[0], jnp.int32)
    for m in range(1, patches):
        step = jnp.where(position >= ends[m - 1], steps[m], step)
    older = step == 1
    for at, cache in enumerate((keys, values)):
        older_rows, newer_rows = cache[1].astype(jnp.float32), cache[0].astype(jnp.float32)
        out[:, at * width : (at + 1) * width] = jnp.where(older, older_rows, newer_rows).astype(jnp.bfloat16)


def pack(out, first, outputs, *stats):
    outputs = outputs.reshape(32, 8, width)
    spread = [jnp.broadcast_to(x, (span, width)).reshape(32, 8, width) for x in stats]
    lane = lax.broadcasted_iota(jnp.int32, (32, 2, width), 2)
    packed = jnp.zeros((32, 2, width), jnp.float32)
    for row in range(4):
        two = slice(2 * row, 2 * row + 2)
        out[pl.ds(first, 32), row] = outputs[:, two, :].astype(jnp.bfloat16)
        for i, x in enumerate(spread):
            packed = jnp.where(lane == 3 * row + i, x[:, two, :], packed)
    out[pl.ds(first, 32), 4] = packed.astype(jnp.bfloat16)


def attend(lengths, queries, fresh, stale, out, *, place):
    za, zb, c = place()
    ends = patch_ends(lengths)
    key_offset = lax.broadcasted_iota(jnp.int32, (span, span), 1)
    row_offset = lax.broadcasted_iota(jnp.int32, (span, 1), 0)

    blocks = []
    for at in range(4):
        rows = pl.ds(at * span, span)
        blocks.append((fresh[rows, :width], fresh[rows, width:], stale[rows, :width], stale[rows, width:], za * 1024 + at * span))

    for at in range(4):
        rows = pl.ds(at * span, span)
        q = queries[rows, :]
        position = at * 1024 + zb * 512 + c * span + row_offset
        reach = jnp.full((span, 1), ends[patches - 1], jnp.int32)
        for m in range(patches - 2, -1, -1):
            reach = jnp.where(position < ends[m], ends[m], reach)
        scores, fresh_at = [], []
        for keys, _, stale_keys, _, first in blocks:
            fresh_scores = lax.dot_general(q, keys, (((1,), (1,)), ((), ())), preferred_element_type=jnp.float32)
            stale_scores = lax.dot_general(q, stale_keys, (((1,), (1,)), ((), ())), preferred_element_type=jnp.float32)
            is_fresh = key_offset < reach - first
            fresh_at.append(is_fresh)
            scores.append(jnp.where(is_fresh, fresh_scores, stale_scores))
        peak = functools.reduce(jnp.maximum, scores)
        peak = jnp.max(peak, axis=1, keepdims=True) * log2_scale
        peak = peak.astype(jnp.bfloat16).astype(jnp.float32)
        weights = [jnp.exp2(s * log2_scale - peak) for s in scores]
        total = jnp.sum(functools.reduce(jnp.add, weights), axis=1, keepdims=True)
        summed = jnp.zeros((span, width), jnp.float32)
        for w, is_fresh, (_, values, _, stale_values, _) in zip(weights, fresh_at, blocks):
            summed += jnp.dot(
                jnp.where(is_fresh, w, 0.0).astype(jnp.bfloat16), values, preferred_element_type=jnp.float32
            )
            summed += jnp.dot(
                jnp.where(is_fresh, 0.0, w).astype(jnp.bfloat16), stale_values, preferred_element_type=jnp.float32
            )
        high = total.astype(jnp.bfloat16).astype(jnp.float32)
        pack(out, at * 32, summed / total, peak, high, total - high)


def combine(parts, out):
    stats = [parts[pl.ds(s * 32, 32), 4].astype(jnp.float32) for s in range(4)]
    joined = []
    for row in range(4):
        peaks, totals = [], []
        for x in stats:
            peaks.append(x[:, :, 3 * row : 3 * row + 1])
            totals.append(x[:, :, 3 * row + 1 : 3 * row + 2] + x[:, :, 3 * row + 2 : 3 * row + 3])
        top = functools.reduce(jnp.maximum, peaks)
        shares = [t * jnp.exp2(p - top) for t, p in zip(totals, peaks)]
        whole = functools.reduce(jnp.add, shares)
        outputs = [parts[pl.ds(s * 32, 32), row].astype(jnp.float32) for s in range(4)]
        joined.append(functools.reduce(jnp.add, [o * (s / whole) for o, s in zip(outputs, shares)]))
    joined = jnp.concatenate(joined, axis=1)
    for h in range(32):
        out[:, h * width : (h + 1) * width] = joined[h].astype(jnp.bfloat16)


def on_device(query, key, value, stale_key, stale_value, patch_lengths, stale_step):
    def place():
        return lax.axis_index(quad), lax.axis_index(pair), lax.axis_index(core)

    def select(lengths, steps, keys, values, out):
        za, zb, c = place()
        pick_stale(lengths, steps, keys, values, out, first=za * 1024 + zb * 512 + c * span)

    swap = [(0, 1), (1, 0)]

    def from_neighbours(x):
        return lax.all_gather(x, (pair, core), axis=0, tiled=True)

    def by_head(x):
        return jnp.transpose(x.reshape(8, 32, width), (1, 0, 2))

    with jax.named_scope("tokens_to_heads"):
        mine = jnp.concatenate([by_head(query), by_head(key), by_head(value)], axis=2)
        mine = lax.all_to_all(mine, head, split_axis=0, concat_axis=0, tiled=True)
        mine = mine.reshape(span, 3 * width)

    with jax.named_scope("stale"):
        stale_own = pl.pallas_call(
            select,
            out_shape=jax.ShapeDtypeStruct((span, 2 * width), jnp.bfloat16),
            in_specs=[whole_smem] * 2 + [whole_vmem] * 2,
            out_specs=whole_vmem,
            compiler_params=small_kernel,
            name="pick_stale",
        )(patch_lengths, stale_step, stale_key, stale_value)
        stale = from_neighbours(stale_own)

    mine, stale = lax.optimization_barrier((mine, stale))

    with jax.named_scope("gather_queries"):
        queries = jnp.broadcast_to(mine[None, :, :width], (4, span, width))
        queries = lax.all_to_all(queries, quad, split_axis=0, concat_axis=0, tiled=True)
        queries = queries.reshape(4 * span, width)

    with jax.named_scope("neighbour_keys"):
        fresh = from_neighbours(mine[:, width:])

    with jax.named_scope("attend"):
        parts = pl.pallas_call(
            functools.partial(attend, place=place),
            out_shape=jax.ShapeDtypeStruct((128, 5, 2, width), jnp.bfloat16),
            in_specs=[whole_smem] + [whole_vmem] * 3,
            out_specs=whole_vmem,
            compiler_params=pltpu.CompilerParams(vmem_limit_bytes=24 << 20),
            cost_estimate=pl.CostEstimate(flops=2 * 2 * 512 * 4096 * 128, bytes_accessed=4 << 20, transcendentals=1 << 20),
            name="attend",
        )(patch_lengths, queries, fresh, stale)

    with jax.named_scope("heads_to_tokens"):
        parts = lax.all_to_all(parts, (quad,) + head, split_axis=0, concat_axis=0, tiled=True)
        return pl.pallas_call(
            combine,
            out_shape=jax.ShapeDtypeStruct((8, 32 * width), jnp.bfloat16),
            in_specs=[whole_vmem],
            out_specs=whole_vmem,
            compiler_params=small_kernel,
            name="combine",
        )(parts)


def solution(mesh):
    fine = Mesh(mesh.devices.reshape(4, 2, 2, 8, 4), (quad, pair, core) + head)
    rows = P(everywhere, None)
    cache = P(None, pipe, head)
    return jax.shard_map(
        on_device,
        mesh=fine,
        in_specs=(rows, rows, rows, cache, cache, P(), P()),
        out_specs=rows,
        check_vma=False,
    )
```

```python
import functools
import math

import jax
import jax.numpy as jnp
from jax import lax
from jax.experimental import pallas as pl
from jax.experimental.pallas import tpu as pltpu
from jax.sharding import Mesh, PartitionSpec as P

width = 128
span = 256
patches = 4
log2_scale = math.log2(math.e) / math.sqrt(width)

quad, pair, core, head = "za", "zb", "core", ("y", "x")
pipe = (quad, pair, core)
everywhere = pipe + head

whole_vmem = pl.BlockSpec(memory_space=pltpu.VMEM)
small_kernel = pltpu.CompilerParams(vmem_limit_bytes=8 << 20)
whole_smem = pl.BlockSpec(memory_space=pltpu.SMEM)


def patch_ends(lengths):
    ends, last = [], 0
    for m in range(patches):
        last = last + lengths[m]
        ends.append(last)
    return ends


def pick_stale(lengths, steps, keys, values, out, *, first):
    ends = patch_ends(lengths)
    position = first + lax.broadcasted_iota(jnp.int32, (span, width), 0)
    step = jnp.full((span, width), steps[0], jnp.int32)
    for m in range(1, patches):
        step = jnp.where(position >= ends[m - 1], steps[m], step)
    older = step == 1
    for at, cache in enumerate((keys, values)):
        older_rows, newer_rows = cache[1].astype(jnp.float32), cache[0].astype(jnp.float32)
        out[:, at * width : (at + 1) * width] = jnp.where(older, older_rows, newer_rows).astype(jnp.bfloat16)


def pack(out, first, outputs, *stats):
    outputs = outputs.reshape(32, 8, width)
    shape = (32, 8, width)
    lane = lax.broadcasted_iota(jnp.int32, shape, 2) - 3 * (lax.broadcasted_iota(jnp.int32, shape, 1) // 2)
    spread = jnp.zeros(shape, jnp.float32)
    for i, x in enumerate(stats):
        spread = jnp.where(lane == i, jnp.broadcast_to(x, (span, width)).reshape(shape), spread)
    packed = spread[:, 0:2] + spread[:, 2:4] + spread[:, 4:6] + spread[:, 6:8]
    rows = pl.ds(first, 32)
    for row in range(4):
        out[rows, row] = outputs[:, 2 * row : 2 * row + 2].astype(jnp.bfloat16)
    out[rows, 4] = packed.astype(jnp.bfloat16)


def row_peak(scores):
    peak = jnp.max(functools.reduce(jnp.maximum, scores), axis=1, keepdims=True) * log2_scale
    return peak.astype(jnp.bfloat16).astype(jnp.float32)


def products(q, keys):
    return lax.dot_general(q, keys, (((1,), (1,)), ((), ())), preferred_element_type=jnp.float32)


def attend(lengths, queries, fresh, stale, out, *, place):
    za, zb, c = place()
    ends = patch_ends(lengths)
    key_first = za * 1024
    parts = [pl.ds(at * span, span) for at in range(4)]

    def reach_of(position):
        reach = ends[patches - 1]
        for m in range(patches - 2, -1, -1):
            reach = jnp.where(position < ends[m], ends[m], reach)
        return reach

    def finish(at, summed, peak, total):
        high = total.astype(jnp.bfloat16).astype(jnp.float32)
        pack(out, at * 32, summed / total, peak, high, total - high)

    def one_version(at, rows):
        q = queries[parts[at], :]
        scores = [products(q, rows[part, :width]) for part in parts]
        peak = row_peak(scores)
        weights = [jnp.exp2(s * log2_scale - peak) for s in scores]
        total = jnp.sum(functools.reduce(jnp.add, weights), axis=1, keepdims=True)
        summed = jnp.zeros((span, width), jnp.float32)
        for w, part in zip(weights, parts):
            summed += jnp.dot(w.astype(jnp.bfloat16), rows[part, width:], preferred_element_type=jnp.float32)
        finish(at, summed, peak, total)

    def both_versions(at, query_first):
        q = queries[parts[at], :]
        reach = reach_of(query_first + lax.broadcasted_iota(jnp.int32, (span, 1), 0))
        offset = lax.broadcasted_iota(jnp.int32, (span, span), 1)
        scores, fresh_at = [], []
        for index, part in enumerate(parts):
            is_fresh = offset < reach - (key_first + index * span)
            fresh_at.append(is_fresh)
            scores.append(jnp.where(is_fresh, products(q, fresh[part, :width]), products(q, stale[part, :width])))
        peak = row_peak(scores)
        weights = [jnp.exp2(s * log2_scale - peak) for s in scores]
        total = jnp.sum(functools.reduce(jnp.add, weights), axis=1, keepdims=True)
        summed = jnp.zeros((span, width), jnp.float32)
        for w, is_fresh, part in zip(weights, fresh_at, parts):
            for version, kept in ((fresh, jnp.where(is_fresh, w, 0.0)), (stale, jnp.where(is_fresh, 0.0, w))):
                summed += jnp.dot(kept.astype(jnp.bfloat16), version[part, width:], preferred_element_type=jnp.float32)
        finish(at, summed, peak, total)

    for at in range(4):
        query_first = at * 1024 + zb * 512 + c * span
        all_fresh = reach_of(query_first) >= key_first + 1024
        all_stale = reach_of(query_first + span - 1) <= key_first
        pl.when(all_fresh)(functools.partial(one_version, at, fresh))
        pl.when(all_stale)(functools.partial(one_version, at, stale))
        pl.when(jnp.logical_not(jnp.logical_or(all_fresh, all_stale)))(functools.partial(both_versions, at, query_first))


def combine(parts, out):
    peaks, totals = [], []
    for s in range(4):
        stats = parts[pl.ds(s * 32, 32), 4].astype(jnp.float32)
        peaks.append(stats)
        totals.append(pltpu.roll(stats, width - 1, 2) + pltpu.roll(stats, width - 2, 2))
    top = functools.reduce(jnp.maximum, peaks)
    shares = [t * jnp.exp2(p - top) for t, p in zip(totals, peaks)]
    scale = 1.0 / functools.reduce(jnp.add, shares)
    shares = [s * scale for s in shares]
    joined = []
    for row in range(4):
        terms = [
            parts[pl.ds(s * 32, 32), row].astype(jnp.float32) * shares[s][:, :, 3 * row : 3 * row + 1] for s in range(4)
        ]
        joined.append(functools.reduce(jnp.add, terms))
    joined = jnp.concatenate(joined, axis=1)
    for h in range(32):
        out[:, h * width : (h + 1) * width] = joined[h].astype(jnp.bfloat16)


def on_device(query, key, value, stale_key, stale_value, patch_lengths, stale_step):
    def place():
        return lax.axis_index(quad), lax.axis_index(pair), lax.axis_index(core)

    def select(lengths, steps, keys, values, out):
        za, zb, c = place()
        pick_stale(lengths, steps, keys, values, out, first=za * 1024 + zb * 512 + c * span)

    swap = [(0, 1), (1, 0)]

    def from_neighbours(x):
        return lax.all_gather(x, (pair, core), axis=0, tiled=True)

    def by_head(x):
        return jnp.transpose(x.reshape(8, 32, width), (1, 0, 2))

    with jax.named_scope("tokens_to_heads"):
        mine = jnp.concatenate([by_head(query), by_head(key), by_head(value)], axis=2)
        mine = lax.all_to_all(mine, head, split_axis=0, concat_axis=0, tiled=True)
        mine = mine.reshape(span, 3 * width)

    with jax.named_scope("stale"):
        stale_own = pl.pallas_call(
            select,
            out_shape=jax.ShapeDtypeStruct((span, 2 * width), jnp.bfloat16),
            in_specs=[whole_smem] * 2 + [whole_vmem] * 2,
            out_specs=whole_vmem,
            compiler_params=small_kernel,
            name="pick_stale",
        )(patch_lengths, stale_step, stale_key, stale_value)
        stale = from_neighbours(stale_own)

    mine, stale = lax.optimization_barrier((mine, stale))

    with jax.named_scope("gather_queries"):
        queries = jnp.broadcast_to(mine[None, :, :width], (4, span, width))
        queries = lax.all_to_all(queries, quad, split_axis=0, concat_axis=0, tiled=True)
        queries = queries.reshape(4 * span, width)

    with jax.named_scope("neighbour_keys"):
        fresh = from_neighbours(mine[:, width:])

    with jax.named_scope("attend"):
        parts = pl.pallas_call(
            functools.partial(attend, place=place),
            out_shape=jax.ShapeDtypeStruct((128, 5, 2, width), jnp.bfloat16),
            in_specs=[whole_smem] + [whole_vmem] * 3,
            out_specs=whole_vmem,
            compiler_params=pltpu.CompilerParams(vmem_limit_bytes=24 << 20),
            cost_estimate=pl.CostEstimate(flops=2 * 2 * 512 * 4096 * 128, bytes_accessed=4 << 20, transcendentals=1 << 20),
            name="attend",
        )(patch_lengths, queries, fresh, stale)

    with jax.named_scope("heads_to_tokens"):
        parts = lax.all_to_all(parts, (quad,) + head, split_axis=0, concat_axis=0, tiled=True)
        return pl.pallas_call(
            combine,
            out_shape=jax.ShapeDtypeStruct((8, 32 * width), jnp.bfloat16),
            in_specs=[whole_vmem],
            out_specs=whole_vmem,
            compiler_params=small_kernel,
            name="combine",
        )(parts)


def solution(mesh):
    fine = Mesh(mesh.devices.reshape(4, 2, 2, 8, 4), (quad, pair, core) + head)
    rows = P(everywhere, None)
    cache = P(None, pipe, head)
    return jax.shard_map(
        on_device,
        mesh=fine,
        in_specs=(rows, rows, rows, cache, cache, P(), P()),
        out_specs=rows,
        check_vma=False,
    )
```

```python
import functools
import math

import jax
import jax.numpy as jnp
from jax import lax
from jax.experimental import pallas as pl
from jax.experimental.pallas import tpu as pltpu
from jax.sharding import Mesh, PartitionSpec as P

width = 128
span = 256
patches = 4
log2_scale = math.log2(math.e) / math.sqrt(width)

quad, pair, core, head = "za", "zb", "core", ("y", "x")
pipe = (quad, pair, core)
everywhere = pipe + head

whole_vmem = pl.BlockSpec(memory_space=pltpu.VMEM)
small_kernel = pltpu.CompilerParams(vmem_limit_bytes=8 << 20)
whole_smem = pl.BlockSpec(memory_space=pltpu.SMEM)


def patch_ends(lengths):
    ends, last = [], 0
    for m in range(patches):
        last = last + lengths[m]
        ends.append(last)
    return ends


def pick_stale(lengths, steps, keys, values, out, *, first):
    ends = patch_ends(lengths)
    position = first + lax.broadcasted_iota(jnp.int32, (span, width), 0)
    step = jnp.full((span, width), steps[0], jnp.int32)
    for m in range(1, patches):
        step = jnp.where(position >= ends[m - 1], steps[m], step)
    older = step == 1
    for at, cache in enumerate((keys, values)):
        older_rows, newer_rows = cache[1].astype(jnp.float32), cache[0].astype(jnp.float32)
        out[:, at * width : (at + 1) * width] = jnp.where(older, older_rows, newer_rows).astype(jnp.bfloat16)


def pack(out, first, outputs, *stats):
    outputs = outputs.reshape(32, 8, width)
    shape = (32, 8, width)
    lane = lax.broadcasted_iota(jnp.int32, shape, 2) - 3 * (lax.broadcasted_iota(jnp.int32, shape, 1) // 2)
    spread = jnp.zeros(shape, jnp.float32)
    for i, x in enumerate(stats):
        spread = jnp.where(lane == i, jnp.broadcast_to(x, (span, width)).reshape(shape), spread)
    packed = spread[:, 0:2] + spread[:, 2:4] + spread[:, 4:6] + spread[:, 6:8]
    rows = pl.ds(first, 32)
    for row in range(4):
        out[rows, row] = outputs[:, 2 * row : 2 * row + 2].astype(jnp.bfloat16)
    out[rows, 4] = packed.astype(jnp.bfloat16)


def row_peak(scores):
    peak = jnp.max(functools.reduce(jnp.maximum, scores), axis=1, keepdims=True) * log2_scale
    return peak.astype(jnp.bfloat16).astype(jnp.float32)


def products(q, keys):
    return lax.dot_general(q, keys, (((1,), (1,)), ((), ())), preferred_element_type=jnp.float32)


def attend(lengths, queries, fresh, stale, *outs, place, aheads):
    for ahead, out in zip(aheads, outs):
        attend_block(lengths, queries, fresh, stale, out, place=place, ahead=ahead)


def attend_block(lengths, queries, fresh, stale, out, *, place, ahead):
    za, zb, c = place()
    ends = patch_ends(lengths)
    key_first = za * 1024
    parts = [pl.ds(at * span, span) for at in range(4)]
    owner = lax.rem(za + ahead, 4)
    query_first = owner * 1024 + zb * 512 + c * span
    query_rows = pl.ds(pl.multiple_of(owner * span, span), span)

    def reach_of(position):
        reach = ends[patches - 1]
        for m in range(patches - 2, -1, -1):
            reach = jnp.where(position < ends[m], ends[m], reach)
        return reach

    def finish(summed, peak, total):
        high = total.astype(jnp.bfloat16).astype(jnp.float32)
        pack(out, 0, summed / total, peak, high, total - high)

    def one_version(rows):
        q = queries[query_rows, :]
        scores = [products(q, rows[part, :width]) for part in parts]
        peak = row_peak(scores)
        weights = [jnp.exp2(s * log2_scale - peak) for s in scores]
        total = jnp.sum(functools.reduce(jnp.add, weights), axis=1, keepdims=True)
        summed = jnp.zeros((span, width), jnp.float32)
        for w, part in zip(weights, parts):
            summed += jnp.dot(w.astype(jnp.bfloat16), rows[part, width:], preferred_element_type=jnp.float32)
        finish(summed, peak, total)

    def both_versions():
        q = queries[query_rows, :]
        reach = reach_of(query_first + lax.broadcasted_iota(jnp.int32, (span, 1), 0))
        offset = lax.broadcasted_iota(jnp.int32, (span, span), 1)
        scores, fresh_at = [], []
        for index, part in enumerate(parts):
            is_fresh = offset < reach - (key_first + index * span)
            fresh_at.append(is_fresh)
            scores.append(jnp.where(is_fresh, products(q, fresh[part, :width]), products(q, stale[part, :width])))
        peak = row_peak(scores)
        weights = [jnp.exp2(s * log2_scale - peak) for s in scores]
        total = jnp.sum(functools.reduce(jnp.add, weights), axis=1, keepdims=True)
        summed = jnp.zeros((span, width), jnp.float32)
        for w, is_fresh, part in zip(weights, fresh_at, parts):
            for version, kept in ((fresh, jnp.where(is_fresh, w, 0.0)), (stale, jnp.where(is_fresh, 0.0, w))):
                summed += jnp.dot(kept.astype(jnp.bfloat16), version[part, width:], preferred_element_type=jnp.float32)
        finish(summed, peak, total)

    all_fresh = reach_of(query_first) >= key_first + 1024
    all_stale = reach_of(query_first + span - 1) <= key_first
    pl.when(all_fresh)(functools.partial(one_version, fresh))
    pl.when(all_stale)(functools.partial(one_version, stale))
    pl.when(jnp.logical_not(jnp.logical_or(all_fresh, all_stale)))(both_versions)


def combine(*refs):
    parts, out = refs[:4], refs[4]
    peaks, totals = [], []
    for part in parts:
        stats = part[:, 4].astype(jnp.float32)
        peaks.append(stats)
        totals.append(pltpu.roll(stats, width - 1, 2) + pltpu.roll(stats, width - 2, 2))
    top = functools.reduce(jnp.maximum, peaks)
    shares = [t * jnp.exp2(p - top) for t, p in zip(totals, peaks)]
    scale = 1.0 / functools.reduce(jnp.add, shares)
    shares = [s * scale for s in shares]
    joined = []
    for row in range(4):
        terms = [part[:, row].astype(jnp.float32) * s[:, :, 3 * row : 3 * row + 1] for part, s in zip(parts, shares)]
        joined.append(functools.reduce(jnp.add, terms))
    out[...] = jnp.concatenate(joined, axis=1).astype(jnp.bfloat16)


def on_device(query, key, value, stale_key, stale_value, patch_lengths, stale_step):
    def place():
        return lax.axis_index(quad), lax.axis_index(pair), lax.axis_index(core)

    def select(lengths, steps, keys, values, out):
        za, zb, c = place()
        pick_stale(lengths, steps, keys, values, out, first=za * 1024 + zb * 512 + c * span)

    swap = [(0, 1), (1, 0)]

    def from_neighbours(x):
        return lax.all_gather(x, (pair, core), axis=0, tiled=True)

    def by_head(x):
        return jnp.transpose(x.reshape(8, 32, width), (1, 0, 2))

    with jax.named_scope("tokens_to_heads"):
        mine = jnp.concatenate([by_head(query), by_head(key), by_head(value)], axis=2)
        mine = lax.all_to_all(mine, head, split_axis=0, concat_axis=0, tiled=True)
        mine = mine.reshape(span, 3 * width)

    with jax.named_scope("stale"):
        stale_own = pl.pallas_call(
            select,
            out_shape=jax.ShapeDtypeStruct((span, 2 * width), jnp.bfloat16),
            in_specs=[whole_smem] * 2 + [whole_vmem] * 2,
            out_specs=whole_vmem,
            compiler_params=small_kernel,
            name="pick_stale",
        )(patch_lengths, stale_step, stale_key, stale_value)
        stale = from_neighbours(stale_own)

    mine, stale = lax.optimization_barrier((mine, stale))

    with jax.named_scope("gather_queries"):
        queries = jnp.broadcast_to(mine[None, :, :width], (4, span, width))
        queries = lax.all_to_all(queries, quad, split_axis=0, concat_axis=0, tiled=True)
        queries = queries.reshape(4 * span, width)

    with jax.named_scope("neighbour_keys"):
        fresh = from_neighbours(mine[:, width:])

    def attend_for(*aheads):
        return pl.pallas_call(
            functools.partial(attend, place=place, aheads=aheads),
            out_shape=[jax.ShapeDtypeStruct((32, 5, 2, width), jnp.bfloat16)] * len(aheads),
            in_specs=[whole_smem] + [whole_vmem] * 3,
            out_specs=[whole_vmem] * len(aheads),
            compiler_params=pltpu.CompilerParams(vmem_limit_bytes=16 << 20),
            cost_estimate=pl.CostEstimate(
                flops=len(aheads) * 2 * 2 * 256 * 2048 * 128, bytes_accessed=2 << 20, transcendentals=len(aheads) << 18
            ),
            name="attend",
        )(patch_lengths, queries, fresh, stale)

    with jax.named_scope("attend_and_send"):
        away = (2, 1, 3)
        parts = [
            lax.ppermute(block, quad, [(i, (i + ahead) % 4) for i in range(4)])
            for ahead, block in zip(away, attend_for(*away))
        ]
        parts += attend_for(0)

    with jax.named_scope("join_partials"):
        joined = pl.pallas_call(
            combine,
            out_shape=jax.ShapeDtypeStruct((32, 8, width), jnp.bfloat16),
            in_specs=[whole_vmem] * 4,
            out_specs=whole_vmem,
            compiler_params=small_kernel,
            name="combine",
        )(*parts)

    with jax.named_scope("heads_to_tokens"):
        joined = lax.all_to_all(joined, head, split_axis=0, concat_axis=0, tiled=True)
        return jnp.transpose(joined, (1, 0, 2)).reshape(8, 32 * width)


def solution(mesh):
    fine = Mesh(mesh.devices.reshape(4, 2, 2, 8, 4), (quad, pair, core) + head)
    rows = P(everywhere, None)
    cache = P(None, pipe, head)
    return jax.shard_map(
        on_device,
        mesh=fine,
        in_specs=(rows, rows, rows, cache, cache, P(), P()),
        out_specs=rows,
        check_vma=False,
    )
```

```python
import functools
import math

import jax
import jax.numpy as jnp
from jax import lax
from jax.experimental import pallas as pl
from jax.experimental.pallas import tpu as pltpu
from jax.sharding import Mesh, PartitionSpec as P

width = 128
span = 256
patches = 4
log2_scale = math.log2(math.e) / math.sqrt(width)

quad, pair, core, head = "za", "zb", "core", ("y", "x")
pipe = (quad, pair, core)
everywhere = pipe + head

whole_vmem = pl.BlockSpec(memory_space=pltpu.VMEM)
small_kernel = pltpu.CompilerParams(vmem_limit_bytes=8 << 20)
whole_smem = pl.BlockSpec(memory_space=pltpu.SMEM)


def patch_ends(lengths):
    ends, last = [], 0
    for m in range(patches):
        last = last + lengths[m]
        ends.append(last)
    return ends


def pick_stale(lengths, steps, keys, values, out, *, first):
    ends = patch_ends(lengths)
    position = first + lax.broadcasted_iota(jnp.int32, (span, width), 0)
    step = jnp.full((span, width), steps[0], jnp.int32)
    for m in range(1, patches):
        step = jnp.where(position >= ends[m - 1], steps[m], step)
    older = step == 1
    for at, cache in enumerate((keys, values)):
        older_rows, newer_rows = cache[1].astype(jnp.float32), cache[0].astype(jnp.float32)
        out[:, at * width : (at + 1) * width] = jnp.where(older, older_rows, newer_rows).astype(jnp.bfloat16)


def pack(out, first, outputs, *stats):
    outputs = outputs.reshape(32, 8, width)
    shape = (32, 8, width)
    lane = lax.broadcasted_iota(jnp.int32, shape, 2) - 3 * (lax.broadcasted_iota(jnp.int32, shape, 1) // 2)
    spread = jnp.zeros(shape, jnp.float32)
    for i, x in enumerate(stats):
        spread = jnp.where(lane == i, jnp.broadcast_to(x, (span, width)).reshape(shape), spread)
    packed = spread[:, 0:2] + spread[:, 2:4] + spread[:, 4:6] + spread[:, 6:8]
    rows = pl.ds(first, 32)
    for row in range(4):
        out[rows, row] = outputs[:, 2 * row : 2 * row + 2].astype(jnp.bfloat16)
    out[rows, 4] = packed.astype(jnp.bfloat16)


def row_peak(scores):
    peak = jnp.max(functools.reduce(jnp.maximum, scores), axis=1, keepdims=True) * log2_scale
    return peak.astype(jnp.bfloat16).astype(jnp.float32)


def products(q, keys):
    return lax.dot_general(q, keys, (((1,), (1,)), ((), ())), preferred_element_type=jnp.float32)


def attend(lengths, queries, fresh, stale, out, *, place):
    za, zb, c = place()
    ends = patch_ends(lengths)
    key_first = za * 1024
    parts = [pl.ds(at * span, span) for at in range(4)]

    def reach_of(position):
        reach = ends[patches - 1]
        for m in range(patches - 2, -1, -1):
            reach = jnp.where(position < ends[m], ends[m], reach)
        return reach

    def finish(at, summed, peak, total):
        high = total.astype(jnp.bfloat16).astype(jnp.float32)
        pack(out, at * 32, summed / total, peak, high, total - high)

    def one_version(at, rows):
        q = queries[parts[at], :]
        scores = [products(q, rows[part, :width]) for part in parts]
        peak = row_peak(scores)
        weights = [jnp.exp2(s * log2_scale - peak) for s in scores]
        total = jnp.sum(functools.reduce(jnp.add, weights), axis=1, keepdims=True)
        summed = jnp.zeros((span, width), jnp.float32)
        for w, part in zip(weights, parts):
            summed += jnp.dot(w.astype(jnp.bfloat16), rows[part, width:], preferred_element_type=jnp.float32)
        finish(at, summed, peak, total)

    def both_versions(at, query_first):
        q = queries[parts[at], :]
        reach = reach_of(query_first + lax.broadcasted_iota(jnp.int32, (span, 1), 0))
        offset = lax.broadcasted_iota(jnp.int32, (span, span), 1)
        scores, fresh_at = [], []
        for index, part in enumerate(parts):
            is_fresh = offset < reach - (key_first + index * span)
            fresh_at.append(is_fresh)
            scores.append(jnp.where(is_fresh, products(q, fresh[part, :width]), products(q, stale[part, :width])))
        peak = row_peak(scores)
        weights = [jnp.exp2(s * log2_scale - peak) for s in scores]
        total = jnp.sum(functools.reduce(jnp.add, weights), axis=1, keepdims=True)
        summed = jnp.zeros((span, width), jnp.float32)
        for w, is_fresh, part in zip(weights, fresh_at, parts):
            for version, kept in ((fresh, jnp.where(is_fresh, w, 0.0)), (stale, jnp.where(is_fresh, 0.0, w))):
                summed += jnp.dot(kept.astype(jnp.bfloat16), version[part, width:], preferred_element_type=jnp.float32)
        finish(at, summed, peak, total)

    for at in range(4):
        query_first = at * 1024 + zb * 512 + c * span
        all_fresh = reach_of(query_first) >= key_first + 1024
        all_stale = reach_of(query_first + span - 1) <= key_first
        pl.when(all_fresh)(functools.partial(one_version, at, fresh))
        pl.when(all_stale)(functools.partial(one_version, at, stale))
        pl.when(jnp.logical_not(jnp.logical_or(all_fresh, all_stale)))(functools.partial(both_versions, at, query_first))


def combine(parts, out):
    lane = lax.broadcasted_iota(jnp.int32, (8, 8, width), 2) - 3 * (lax.broadcasted_iota(jnp.int32, (8, 8, width), 1) // 2)
    blocks = [parts[pl.ds(s * 320, 320), :].astype(jnp.float32).reshape(8, 40, width) for s in range(4)]
    for j in range(4):
        stats = [x[:, 10 * j + 8 : 10 * j + 10] for x in blocks]
        totals = [pltpu.roll(x, width - 1, 2) + pltpu.roll(x, width - 2, 2) for x in stats]
        top = functools.reduce(jnp.maximum, stats)
        shares = [t * jnp.exp2(p - top) for t, p in zip(totals, stats)]
        scale = 1.0 / functools.reduce(jnp.add, shares)
        joined = jnp.zeros((8, 8, width), jnp.float32)
        for x, share in zip(blocks, shares):
            share = share * scale
            share = jnp.concatenate([share] * 4, axis=1)
            share = jnp.sum(jnp.where(lane == 0, share, 0.0), axis=2, keepdims=True)
            joined += x[:, 10 * j : 10 * j + 8] * share
        joined = joined.astype(jnp.bfloat16)
        for g in range(8):
            h = 4 * g + j
            out[:, h * width : (h + 1) * width] = joined[g]


def on_device(query, key, value, stale_key, stale_value, patch_lengths, stale_step):
    def place():
        return lax.axis_index(quad), lax.axis_index(pair), lax.axis_index(core)

    def select(lengths, steps, keys, values, out):
        za, zb, c = place()
        pick_stale(lengths, steps, keys, values, out, first=za * 1024 + zb * 512 + c * span)

    swap = [(0, 1), (1, 0)]

    def from_neighbours(x):
        return lax.all_gather(x, (pair, core), axis=0, tiled=True)

    def by_head(x):
        return jnp.transpose(x.reshape(8, 32, width), (1, 0, 2))

    with jax.named_scope("tokens_to_heads"):
        mine = jnp.concatenate([by_head(query), by_head(key), by_head(value)], axis=2)
        mine = lax.all_to_all(mine, head, split_axis=0, concat_axis=0, tiled=True)
        mine = mine.reshape(span, 3 * width)

    with jax.named_scope("stale"):
        stale_own = pl.pallas_call(
            select,
            out_shape=jax.ShapeDtypeStruct((span, 2 * width), jnp.bfloat16),
            in_specs=[whole_smem] * 2 + [whole_vmem] * 2,
            out_specs=whole_vmem,
            compiler_params=small_kernel,
            name="pick_stale",
        )(patch_lengths, stale_step, stale_key, stale_value)
        stale = from_neighbours(stale_own)

    mine, stale = lax.optimization_barrier((mine, stale))

    with jax.named_scope("gather_queries"):
        queries = jnp.broadcast_to(mine[None, :, :width], (4, span, width))
        queries = lax.all_to_all(queries, quad, split_axis=0, concat_axis=0, tiled=True)
        queries = queries.reshape(4 * span, width)

    with jax.named_scope("neighbour_keys"):
        fresh = from_neighbours(mine[:, width:])

    with jax.named_scope("attend"):
        parts = pl.pallas_call(
            functools.partial(attend, place=place),
            out_shape=jax.ShapeDtypeStruct((128, 5, 2, width), jnp.bfloat16),
            in_specs=[whole_smem] + [whole_vmem] * 3,
            out_specs=whole_vmem,
            compiler_params=pltpu.CompilerParams(vmem_limit_bytes=24 << 20),
            cost_estimate=pl.CostEstimate(flops=2 * 2 * 512 * 4096 * 128, bytes_accessed=4 << 20, transcendentals=1 << 20),
            name="attend",
        )(patch_lengths, queries, fresh, stale)

    with jax.named_scope("heads_to_tokens"):
        parts = lax.all_to_all(parts, (quad,) + head, split_axis=0, concat_axis=0, tiled=True)
        return pl.pallas_call(
            combine,
            out_shape=jax.ShapeDtypeStruct((8, 32 * width), jnp.bfloat16),
            in_specs=[whole_vmem],
            out_specs=whole_vmem,
            compiler_params=small_kernel,
            name="combine",
        )(parts.reshape(1280, width))


def solution(mesh):
    fine = Mesh(mesh.devices.reshape(4, 2, 2, 8, 4), (quad, pair, core) + head)
    rows = P(everywhere, None)
    cache = P(None, pipe, head)
    return jax.shard_map(
        on_device,
        mesh=fine,
        in_specs=(rows, rows, rows, cache, cache, P(), P()),
        out_specs=rows,
        check_vma=False,
    )
```

```python
import functools
import math

import jax
import jax.numpy as jnp
from jax import lax
from jax.experimental import pallas as pl
from jax.experimental.pallas import tpu as pltpu
from jax.sharding import Mesh, PartitionSpec as P

width = 128
span = 256
patches = 4
log2_scale = math.log2(math.e) / math.sqrt(width)

quad, pair, core, head = "za", "zb", "core", ("y", "x")
pipe = (quad, pair, core)
everywhere = pipe + head

whole_vmem = pl.BlockSpec(memory_space=pltpu.VMEM)
small_kernel = pltpu.CompilerParams(vmem_limit_bytes=8 << 20)
whole_smem = pl.BlockSpec(memory_space=pltpu.SMEM)


def patch_ends(lengths):
    ends, last = [], 0
    for m in range(patches):
        last = last + lengths[m]
        ends.append(last)
    return ends


def pick_stale(lengths, steps, keys, values, out, *, first):
    ends = patch_ends(lengths)
    position = first + lax.broadcasted_iota(jnp.int32, (span, width), 0)
    step = jnp.full((span, width), steps[0], jnp.int32)
    for m in range(1, patches):
        step = jnp.where(position >= ends[m - 1], steps[m], step)
    older = step == 1
    for at, cache in enumerate((keys, values)):
        older_rows, newer_rows = cache[1].astype(jnp.float32), cache[0].astype(jnp.float32)
        out[:, at * width : (at + 1) * width] = jnp.where(older, older_rows, newer_rows).astype(jnp.bfloat16)


def pack(out, first, outputs, *stats):
    outputs = outputs.reshape(32, 8, width)
    shape = (32, 8, width)
    lane = lax.broadcasted_iota(jnp.int32, shape, 2) - 3 * (lax.broadcasted_iota(jnp.int32, shape, 1) // 2)
    spread = jnp.zeros(shape, jnp.float32)
    for i, x in enumerate(stats):
        spread = jnp.where(lane == i, jnp.broadcast_to(x, (span, width)).reshape(shape), spread)
    packed = spread[:, 0:2] + spread[:, 2:4] + spread[:, 4:6] + spread[:, 6:8]
    rows = pl.ds(first, 32)
    for row in range(4):
        out[rows, row] = outputs[:, 2 * row : 2 * row + 2].astype(jnp.bfloat16)
    out[rows, 4] = packed.astype(jnp.bfloat16)


def row_peak(scores):
    peak = jnp.max(functools.reduce(jnp.maximum, scores), axis=1, keepdims=True) * log2_scale
    return peak.astype(jnp.bfloat16).astype(jnp.float32)


def products(q, keys):
    return lax.dot_general(q, keys, (((1,), (1,)), ((), ())), preferred_element_type=jnp.float32)


def attend(lengths, queries, fresh, stale, out, merged, *, place):
    za, zb, c = place()
    ends = patch_ends(lengths)
    key_first = za * 1024
    parts = [pl.ds(at * span, span) for at in range(4)]

    def reach_of(position):
        reach = ends[patches - 1]
        for m in range(patches - 2, -1, -1):
            reach = jnp.where(position < ends[m], ends[m], reach)
        return reach

    def finish(at, summed, peak, total):
        high = total.astype(jnp.bfloat16).astype(jnp.float32)
        pack(out, at * 32, summed / total, peak, high, total - high)

    def one_version(at, rows):
        q = queries[pl.ds(pl.multiple_of(at * span, span), span), :]
        scores = [products(q, rows[part, :width]) for part in parts]
        peak = row_peak(scores)
        weights = [jnp.exp2(s * log2_scale - peak) for s in scores]
        total = jnp.sum(functools.reduce(jnp.add, weights), axis=1, keepdims=True)
        summed = jnp.zeros((span, width), jnp.float32)
        for w, part in zip(weights, parts):
            summed += jnp.dot(w.astype(jnp.bfloat16), rows[part, width:], preferred_element_type=jnp.float32)
        finish(at, summed, peak, total)

    def both_versions(at, query_first):
        q = queries[pl.ds(pl.multiple_of(at * span, span), span), :]
        reach = reach_of(query_first + lax.broadcasted_iota(jnp.int32, (span, 1), 0))
        offset = lax.broadcasted_iota(jnp.int32, (span, span), 1)
        scores, fresh_at = [], []
        for index, part in enumerate(parts):
            is_fresh = offset < reach - (key_first + index * span)
            fresh_at.append(is_fresh)
            scores.append(jnp.where(is_fresh, products(q, fresh[part, :width]), products(q, stale[part, :width])))
        peak = row_peak(scores)
        weights = [jnp.exp2(s * log2_scale - peak) for s in scores]
        total = jnp.sum(functools.reduce(jnp.add, weights), axis=1, keepdims=True)
        summed = jnp.zeros((span, width), jnp.float32)
        for w, is_fresh, part in zip(weights, fresh_at, parts):
            for version, kept in ((fresh, jnp.where(is_fresh, w, 0.0)), (stale, jnp.where(is_fresh, 0.0, w))):
                summed += jnp.dot(kept.astype(jnp.bfloat16), version[part, width:], preferred_element_type=jnp.float32)
        finish(at, summed, peak, total)

    def merge(reach):
        position = key_first + lax.broadcasted_iota(jnp.int32, (span, 2 * width), 0)
        for index, part in enumerate(parts):
            chosen = jnp.where(position + index * span < reach, fresh[part].astype(jnp.float32), stale[part].astype(jnp.float32))
            merged[part] = chosen.astype(jnp.bfloat16)

    @pl.loop(0, 4)
    def one_block(at):
        query_first = at * 1024 + zb * 512 + c * span
        least, most = reach_of(query_first), reach_of(query_first + span - 1)
        all_fresh = least >= key_first + 1024
        all_stale = most <= key_first
        some = jnp.logical_not(jnp.logical_or(all_fresh, all_stale))
        alike = least == most

        @pl.when(all_fresh)
        def fresh_only():
            one_version(at, fresh)

        @pl.when(all_stale)
        def stale_only():
            one_version(at, stale)

        @pl.when(jnp.logical_and(some, alike))
        def one_boundary():
            merge(least)
            one_version(at, merged)

        @pl.when(jnp.logical_and(some, jnp.logical_not(alike)))
        def several_boundaries():
            both_versions(at, query_first)


def combine(parts, out):
    lane = lax.broadcasted_iota(jnp.int32, (8, 8, width), 2) - 3 * (lax.broadcasted_iota(jnp.int32, (8, 8, width), 1) // 2)
    blocks = [parts[pl.ds(s * 320, 320), :].astype(jnp.float32).reshape(8, 40, width) for s in range(4)]
    for j in range(4):
        stats = [x[:, 10 * j + 8 : 10 * j + 10] for x in blocks]
        totals = [pltpu.roll(x, width - 1, 2) + pltpu.roll(x, width - 2, 2) for x in stats]
        top = functools.reduce(jnp.maximum, stats)
        shares = [t * jnp.exp2(p - top) for t, p in zip(totals, stats)]
        scale = 1.0 / functools.reduce(jnp.add, shares)
        joined = jnp.zeros((8, 8, width), jnp.float32)
        for x, share in zip(blocks, shares):
            share = share * scale
            share = jnp.concatenate([share] * 4, axis=1)
            share = jnp.sum(jnp.where(lane == 0, share, 0.0), axis=2, keepdims=True)
            joined += x[:, 10 * j : 10 * j + 8] * share
        joined = joined.astype(jnp.bfloat16)
        for g in range(8):
            h = 4 * g + j
            out[:, h * width : (h + 1) * width] = joined[g]


def on_device(query, key, value, stale_key, stale_value, patch_lengths, stale_step):
    def place():
        return lax.axis_index(quad), lax.axis_index(pair), lax.axis_index(core)

    def select(lengths, steps, keys, values, out):
        za, zb, c = place()
        pick_stale(lengths, steps, keys, values, out, first=za * 1024 + zb * 512 + c * span)

    swap = [(0, 1), (1, 0)]

    def from_neighbours(x):
        return lax.all_gather(x, (pair, core), axis=0, tiled=True)

    def by_head(x):
        return jnp.transpose(x.reshape(8, 32, width), (1, 0, 2))

    with jax.named_scope("tokens_to_heads"):
        mine = jnp.concatenate([by_head(query), by_head(key), by_head(value)], axis=2)
        mine = lax.all_to_all(mine, head, split_axis=0, concat_axis=0, tiled=True)
        mine = mine.reshape(span, 3 * width)

    with jax.named_scope("stale"):
        stale_own = pl.pallas_call(
            select,
            out_shape=jax.ShapeDtypeStruct((span, 2 * width), jnp.bfloat16),
            in_specs=[whole_smem] * 2 + [whole_vmem] * 2,
            out_specs=whole_vmem,
            compiler_params=small_kernel,
            name="pick_stale",
        )(patch_lengths, stale_step, stale_key, stale_value)
        stale = from_neighbours(stale_own)

    mine, stale = lax.optimization_barrier((mine, stale))

    with jax.named_scope("gather_queries"):
        queries = jnp.broadcast_to(mine[None, :, :width], (4, span, width))
        queries = lax.all_to_all(queries, quad, split_axis=0, concat_axis=0, tiled=True)
        queries = queries.reshape(4 * span, width)

    with jax.named_scope("neighbour_keys"):
        fresh = from_neighbours(mine[:, width:])

    with jax.named_scope("attend"):
        parts = pl.pallas_call(
            functools.partial(attend, place=place),
            out_shape=jax.ShapeDtypeStruct((128, 5, 2, width), jnp.bfloat16),
            in_specs=[whole_smem] + [whole_vmem] * 3,
            out_specs=whole_vmem,
            scratch_shapes=[pltpu.VMEM((4 * span, 2 * width), jnp.bfloat16)],
            compiler_params=pltpu.CompilerParams(vmem_limit_bytes=24 << 20),
            cost_estimate=pl.CostEstimate(flops=2 * 2 * 512 * 4096 * 128, bytes_accessed=4 << 20, transcendentals=1 << 20),
            name="attend",
        )(patch_lengths, queries, fresh, stale)

    with jax.named_scope("heads_to_tokens"):
        parts = lax.all_to_all(parts, (quad,) + head, split_axis=0, concat_axis=0, tiled=True)
        return pl.pallas_call(
            combine,
            out_shape=jax.ShapeDtypeStruct((8, 32 * width), jnp.bfloat16),
            in_specs=[whole_vmem],
            out_specs=whole_vmem,
            compiler_params=small_kernel,
            name="combine",
        )(parts.reshape(1280, width))


def solution(mesh):
    fine = Mesh(mesh.devices.reshape(4, 2, 2, 8, 4), (quad, pair, core) + head)
    rows = P(everywhere, None)
    cache = P(None, pipe, head)
    return jax.shard_map(
        on_device,
        mesh=fine,
        in_specs=(rows, rows, rows, cache, cache, P(), P()),
        out_specs=rows,
        check_vma=False,
    )
```

```python
import functools
import math

import jax
import jax.numpy as jnp
from jax import lax
from jax.experimental import pallas as pl
from jax.experimental.pallas import tpu as pltpu
from jax.sharding import Mesh, PartitionSpec as P

width = 128
span = 256
patches = 4
log2_scale = math.log2(math.e) / math.sqrt(width)

quad, pair, core, head = "za", "zb", "core", ("y", "x")
pipe = (quad, pair, core)
everywhere = pipe + head

whole_vmem = pl.BlockSpec(memory_space=pltpu.VMEM)
small_kernel = pltpu.CompilerParams(vmem_limit_bytes=8 << 20)
whole_smem = pl.BlockSpec(memory_space=pltpu.SMEM)


def patch_ends(lengths):
    ends, last = [], 0
    for m in range(patches):
        last = last + lengths[m]
        ends.append(last)
    return ends


def prepare(lengths, steps, query, key, value, stale_keys, stale_values, mine, stale, *, place):
    for at, tokens in enumerate((query, key, value)):
        for h in range(32):
            mine[h, :, at * width : (at + 1) * width] = tokens[:, h * width : (h + 1) * width]

    za, zb, c = place()
    ends = patch_ends(lengths)
    position = za * 1024 + zb * 512 + c * span + lax.broadcasted_iota(jnp.int32, (span, width), 0)
    step = jnp.full((span, width), steps[0], jnp.int32)
    for m in range(1, patches):
        step = jnp.where(position >= ends[m - 1], steps[m], step)
    older = step == 1
    for at, cache in enumerate((stale_keys, stale_values)):
        chosen = jnp.where(older, cache[1].astype(jnp.float32), cache[0].astype(jnp.float32))
        stale[:, at * width : (at + 1) * width] = chosen.astype(jnp.bfloat16)


def pack(out, first, outputs, *stats):
    outputs = outputs.reshape(32, 8, width)
    shape = (32, 8, width)
    lane = lax.broadcasted_iota(jnp.int32, shape, 2) - 3 * (lax.broadcasted_iota(jnp.int32, shape, 1) // 2)
    spread = jnp.zeros(shape, jnp.float32)
    for i, x in enumerate(stats):
        spread = jnp.where(lane == i, jnp.broadcast_to(x, (span, width)).reshape(shape), spread)
    packed = spread[:, 0:2] + spread[:, 2:4] + spread[:, 4:6] + spread[:, 6:8]
    rows = pl.ds(first, 32)
    for row in range(4):
        out[rows, row] = outputs[:, 2 * row : 2 * row + 2].astype(jnp.bfloat16)
    out[rows, 4] = packed.astype(jnp.bfloat16)


def row_peak(scores):
    peak = jnp.max(functools.reduce(jnp.maximum, scores), axis=1, keepdims=True) * log2_scale
    return peak.astype(jnp.bfloat16).astype(jnp.float32)


def products(q, keys):
    return lax.dot_general(q, keys, (((1,), (1,)), ((), ())), preferred_element_type=jnp.float32)


def attend(lengths, queries, fresh, stale, out, merged, *, place):
    za, zb, c = place()
    ends = patch_ends(lengths)
    key_first = za * 1024
    parts = [pl.ds(at * span, span) for at in range(4)]

    def reach_of(position):
        reach = ends[patches - 1]
        for m in range(patches - 2, -1, -1):
            reach = jnp.where(position < ends[m], ends[m], reach)
        return reach

    def finish(at, summed, peak, total):
        high = total.astype(jnp.bfloat16).astype(jnp.float32)
        pack(out, at * 32, summed / total, peak, high, total - high)

    def one_version(at, rows):
        q = queries[pl.ds(pl.multiple_of(at * span, span), span), :]
        scores = [products(q, rows[part, :width]) for part in parts]
        peak = row_peak(scores)
        weights = [jnp.exp2(s * log2_scale - peak) for s in scores]
        total = jnp.sum(functools.reduce(jnp.add, weights), axis=1, keepdims=True)
        summed = jnp.zeros((span, width), jnp.float32)
        for w, part in zip(weights, parts):
            summed += jnp.dot(w.astype(jnp.bfloat16), rows[part, width:], preferred_element_type=jnp.float32)
        finish(at, summed, peak, total)

    def both_versions(at, query_first):
        q = queries[pl.ds(pl.multiple_of(at * span, span), span), :]
        reach = reach_of(query_first + lax.broadcasted_iota(jnp.int32, (span, 1), 0))
        offset = lax.broadcasted_iota(jnp.int32, (span, span), 1)
        scores, fresh_at = [], []
        for index, part in enumerate(parts):
            is_fresh = offset < reach - (key_first + index * span)
            fresh_at.append(is_fresh)
            scores.append(jnp.where(is_fresh, products(q, fresh[part, :width]), products(q, stale[part, :width])))
        peak = row_peak(scores)
        weights = [jnp.exp2(s * log2_scale - peak) for s in scores]
        total = jnp.sum(functools.reduce(jnp.add, weights), axis=1, keepdims=True)
        summed = jnp.zeros((span, width), jnp.float32)
        for w, is_fresh, part in zip(weights, fresh_at, parts):
            for version, kept in ((fresh, jnp.where(is_fresh, w, 0.0)), (stale, jnp.where(is_fresh, 0.0, w))):
                summed += jnp.dot(kept.astype(jnp.bfloat16), version[part, width:], preferred_element_type=jnp.float32)
        finish(at, summed, peak, total)

    def merge(reach):
        position = key_first + lax.broadcasted_iota(jnp.int32, (span, 2 * width), 0)
        for index, part in enumerate(parts):
            chosen = jnp.where(position + index * span < reach, fresh[part].astype(jnp.float32), stale[part].astype(jnp.float32))
            merged[part] = chosen.astype(jnp.bfloat16)

    @pl.loop(0, 4)
    def one_block(at):
        query_first = at * 1024 + zb * 512 + c * span
        least, most = reach_of(query_first), reach_of(query_first + span - 1)
        all_fresh = least >= key_first + 1024
        all_stale = most <= key_first
        some = jnp.logical_not(jnp.logical_or(all_fresh, all_stale))
        alike = least == most

        @pl.when(all_fresh)
        def fresh_only():
            one_version(at, fresh)

        @pl.when(all_stale)
        def stale_only():
            one_version(at, stale)

        @pl.when(jnp.logical_and(some, alike))
        def one_boundary():
            merge(least)
            one_version(at, merged)

        @pl.when(jnp.logical_and(some, jnp.logical_not(alike)))
        def several_boundaries():
            both_versions(at, query_first)


def combine(parts, out):
    lane = lax.broadcasted_iota(jnp.int32, (8, 8, width), 2) - 3 * (lax.broadcasted_iota(jnp.int32, (8, 8, width), 1) // 2)
    blocks = [parts[pl.ds(s * 320, 320), :].astype(jnp.float32).reshape(8, 40, width) for s in range(4)]
    for j in range(4):
        stats = [x[:, 10 * j + 8 : 10 * j + 10] for x in blocks]
        totals = [pltpu.roll(x, width - 1, 2) + pltpu.roll(x, width - 2, 2) for x in stats]
        top = functools.reduce(jnp.maximum, stats)
        shares = [t * jnp.exp2(p - top) for t, p in zip(totals, stats)]
        scale = 1.0 / functools.reduce(jnp.add, shares)
        joined = jnp.zeros((8, 8, width), jnp.float32)
        for x, share in zip(blocks, shares):
            share = share * scale
            share = jnp.concatenate([share] * 4, axis=1)
            share = jnp.sum(jnp.where(lane == 0, share, 0.0), axis=2, keepdims=True)
            joined += x[:, 10 * j : 10 * j + 8] * share
        joined = joined.astype(jnp.bfloat16)
        for g in range(8):
            h = 4 * g + j
            out[:, h * width : (h + 1) * width] = joined[g]


def on_device(query, key, value, stale_key, stale_value, patch_lengths, stale_step):
    def place():
        return lax.axis_index(quad), lax.axis_index(pair), lax.axis_index(core)

    def from_neighbours(x):
        return lax.all_gather(x, (pair, core), axis=0, tiled=True)

    with jax.named_scope("prepare"):
        mine, stale_own = pl.pallas_call(
            functools.partial(prepare, place=place),
            out_shape=[
                jax.ShapeDtypeStruct((32, 8, 3 * width), jnp.bfloat16),
                jax.ShapeDtypeStruct((span, 2 * width), jnp.bfloat16),
            ],
            in_specs=[whole_smem] * 2 + [whole_vmem] * 5,
            out_specs=[whole_vmem] * 2,
            name="prepare",
        )(patch_lengths, stale_step, query, key, value, stale_key, stale_value)

    with jax.named_scope("tokens_to_heads"):
        mine = lax.all_to_all(mine, head, split_axis=0, concat_axis=0, tiled=True)
        mine = mine.reshape(span, 3 * width)

    with jax.named_scope("stale"):
        stale = from_neighbours(stale_own)

    mine, stale = lax.optimization_barrier((mine, stale))

    with jax.named_scope("gather_queries"):
        queries = jnp.broadcast_to(mine[None, :, :width], (4, span, width))
        queries = lax.all_to_all(queries, quad, split_axis=0, concat_axis=0, tiled=True)
        queries = queries.reshape(4 * span, width)

    with jax.named_scope("neighbour_keys"):
        fresh = from_neighbours(mine[:, width:])

    with jax.named_scope("attend"):
        parts = pl.pallas_call(
            functools.partial(attend, place=place),
            out_shape=jax.ShapeDtypeStruct((128, 5, 2, width), jnp.bfloat16),
            in_specs=[whole_smem] + [whole_vmem] * 3,
            out_specs=whole_vmem,
            scratch_shapes=[pltpu.VMEM((4 * span, 2 * width), jnp.bfloat16)],
            compiler_params=pltpu.CompilerParams(vmem_limit_bytes=24 << 20),
            cost_estimate=pl.CostEstimate(flops=2 * 2 * 512 * 4096 * 128, bytes_accessed=4 << 20, transcendentals=1 << 20),
            name="attend",
        )(patch_lengths, queries, fresh, stale)

    with jax.named_scope("heads_to_tokens"):
        parts = lax.all_to_all(parts, (quad,) + head, split_axis=0, concat_axis=0, tiled=True)
        return pl.pallas_call(
            combine,
            out_shape=jax.ShapeDtypeStruct((8, 32 * width), jnp.bfloat16),
            in_specs=[whole_vmem],
            out_specs=whole_vmem,
            compiler_params=small_kernel,
            name="combine",
        )(parts.reshape(1280, width))


def solution(mesh):
    fine = Mesh(mesh.devices.reshape(4, 2, 2, 8, 4), (quad, pair, core) + head)
    rows = P(everywhere, None)
    cache = P(None, pipe, head)
    return jax.shard_map(
        on_device,
        mesh=fine,
        in_specs=(rows, rows, rows, cache, cache, P(), P()),
        out_specs=rows,
        check_vma=False,
    )
```

```python
import functools
import math

import jax
import jax.numpy as jnp
from jax import lax
from jax.experimental import pallas as pl
from jax.experimental.pallas import tpu as pltpu
from jax.sharding import Mesh, PartitionSpec as P

width = 128
span = 256
patches = 4
log2_scale = math.log2(math.e) / math.sqrt(width)

quad, pair, core, head = "za", "zb", "core", ("y", "x")
pipe = (quad, pair, core)
everywhere = pipe + head

whole_vmem = pl.BlockSpec(memory_space=pltpu.VMEM)
small_kernel = pltpu.CompilerParams(vmem_limit_bytes=8 << 20)
whole_smem = pl.BlockSpec(memory_space=pltpu.SMEM)


def patch_ends(lengths):
    ends, last = [], 0
    for m in range(patches):
        last = last + lengths[m]
        ends.append(last)
    return ends


def pick_stale(lengths, steps, keys, values, out, *, first):
    ends = patch_ends(lengths)
    position = first + lax.broadcasted_iota(jnp.int32, (span, width), 0)
    step = jnp.full((span, width), steps[0], jnp.int32)
    for m in range(1, patches):
        step = jnp.where(position >= ends[m - 1], steps[m], step)
    older = step == 1
    for at, cache in enumerate((keys, values)):
        older_rows, newer_rows = cache[1].astype(jnp.float32), cache[0].astype(jnp.float32)
        out[:, at * width : (at + 1) * width] = jnp.where(older, older_rows, newer_rows).astype(jnp.bfloat16)


def pack(out, first, outputs, *stats):
    outputs = outputs.reshape(32, 8, width)
    shape = (32, 8, width)
    lane = lax.broadcasted_iota(jnp.int32, shape, 2) - 3 * (lax.broadcasted_iota(jnp.int32, shape, 1) // 2)
    spread = jnp.zeros(shape, jnp.float32)
    for i, x in enumerate(stats):
        spread = jnp.where(lane == i, jnp.broadcast_to(x, (span, width)).reshape(shape), spread)
    packed = spread[:, 0:2] + spread[:, 2:4] + spread[:, 4:6] + spread[:, 6:8]
    rows = pl.ds(first, 32)
    for row in range(4):
        out[rows, row] = outputs[:, 2 * row : 2 * row + 2].astype(jnp.bfloat16)
    out[rows, 4] = packed.astype(jnp.bfloat16)


def row_peak(scores):
    peak = jnp.max(functools.reduce(jnp.maximum, scores), axis=1, keepdims=True) * log2_scale
    return peak.astype(jnp.bfloat16).astype(jnp.float32)


def products(q, keys):
    return lax.dot_general(q, keys, (((1,), (1,)), ((), ())), preferred_element_type=jnp.float32)


def attend(lengths, queries, fresh, stale, out, merged, *, place):
    za, zb, c = place()
    ends = patch_ends(lengths)
    key_first = za * 1024
    parts = [pl.ds(at * span, span) for at in range(4)]

    def reach_of(position):
        reach = ends[patches - 1]
        for m in range(patches - 2, -1, -1):
            reach = jnp.where(position < ends[m], ends[m], reach)
        return reach

    def finish(at, summed, peak, total):
        high = total.astype(jnp.bfloat16).astype(jnp.float32)
        pack(out, at * 32, summed / total, peak, high, total - high)

    def one_version(at, rows):
        q = queries[pl.ds(pl.multiple_of(at * span, span), span), :]
        scores = [products(q, rows[part, :width]) for part in parts]
        peak = row_peak(scores)
        weights = [jnp.exp2(s * log2_scale - peak) for s in scores]
        total = jnp.sum(functools.reduce(jnp.add, weights), axis=1, keepdims=True)
        summed = jnp.zeros((span, width), jnp.float32)
        for w, part in zip(weights, parts):
            summed += jnp.dot(w.astype(jnp.bfloat16), rows[part, width:], preferred_element_type=jnp.float32)
        finish(at, summed, peak, total)

    def both_versions(at, query_first):
        q = queries[pl.ds(pl.multiple_of(at * span, span), span), :]
        reach = reach_of(query_first + lax.broadcasted_iota(jnp.int32, (span, 1), 0))
        offset = lax.broadcasted_iota(jnp.int32, (span, span), 1)
        scores, fresh_at = [], []
        for index, part in enumerate(parts):
            is_fresh = offset < reach - (key_first + index * span)
            fresh_at.append(is_fresh)
            scores.append(jnp.where(is_fresh, products(q, fresh[part, :width]), products(q, stale[part, :width])))
        peak = row_peak(scores)
        weights = [jnp.exp2(s * log2_scale - peak) for s in scores]
        total = jnp.sum(functools.reduce(jnp.add, weights), axis=1, keepdims=True)
        summed = jnp.zeros((span, width), jnp.float32)
        for w, is_fresh, part in zip(weights, fresh_at, parts):
            for version, kept in ((fresh, jnp.where(is_fresh, w, 0.0)), (stale, jnp.where(is_fresh, 0.0, w))):
                summed += jnp.dot(kept.astype(jnp.bfloat16), version[part, width:], preferred_element_type=jnp.float32)
        finish(at, summed, peak, total)

    def merge(reach):
        position = key_first + lax.broadcasted_iota(jnp.int32, (span, 2 * width), 0)
        for index, part in enumerate(parts):
            merged[part] = jnp.where(position + index * span < reach, fresh[part], stale[part])

    @pl.loop(0, 4)
    def one_block(at):
        query_first = at * 1024 + zb * 512 + c * span
        least, most = reach_of(query_first), reach_of(query_first + span - 1)
        all_fresh = least >= key_first + 1024
        all_stale = most <= key_first
        some = jnp.logical_not(jnp.logical_or(all_fresh, all_stale))
        alike = least == most

        @pl.when(all_fresh)
        def fresh_only():
            one_version(at, fresh)

        @pl.when(all_stale)
        def stale_only():
            one_version(at, stale)

        @pl.when(jnp.logical_and(some, alike))
        def one_boundary():
            merge(least)
            one_version(at, merged)

        @pl.when(jnp.logical_and(some, jnp.logical_not(alike)))
        def several_boundaries():
            both_versions(at, query_first)


def combine(parts, out):
    lane = lax.broadcasted_iota(jnp.int32, (8, 8, width), 2) - 3 * (lax.broadcasted_iota(jnp.int32, (8, 8, width), 1) // 2)
    blocks = [parts[pl.ds(s * 320, 320), :].astype(jnp.float32).reshape(8, 40, width) for s in range(4)]
    for j in range(4):
        stats = [x[:, 10 * j + 8 : 10 * j + 10] for x in blocks]
        totals = [pltpu.roll(x, width - 1, 2) + pltpu.roll(x, width - 2, 2) for x in stats]
        top = functools.reduce(jnp.maximum, stats)
        shares = [t * jnp.exp2(p - top) for t, p in zip(totals, stats)]
        scale = 1.0 / functools.reduce(jnp.add, shares)
        joined = jnp.zeros((8, 8, width), jnp.float32)
        for x, share in zip(blocks, shares):
            share = share * scale
            share = jnp.concatenate([share] * 4, axis=1)
            share = jnp.sum(jnp.where(lane == 0, share, 0.0), axis=2, keepdims=True)
            joined += x[:, 10 * j : 10 * j + 8] * share
        joined = joined.astype(jnp.bfloat16)
        for g in range(8):
            h = 4 * g + j
            out[:, h * width : (h + 1) * width] = joined[g]


def on_device(query, key, value, stale_key, stale_value, patch_lengths, stale_step):
    def place():
        return lax.axis_index(quad), lax.axis_index(pair), lax.axis_index(core)

    def select(lengths, steps, keys, values, out):
        za, zb, c = place()
        pick_stale(lengths, steps, keys, values, out, first=za * 1024 + zb * 512 + c * span)

    swap = [(0, 1), (1, 0)]

    def from_neighbours(x):
        return lax.all_gather(x, (pair, core), axis=0, tiled=True)

    def by_head(x):
        return jnp.transpose(x.reshape(8, 32, width), (1, 0, 2))

    with jax.named_scope("tokens_to_heads"):
        mine = jnp.concatenate([by_head(query), by_head(key), by_head(value)], axis=2)
        mine = lax.all_to_all(mine, head, split_axis=0, concat_axis=0, tiled=True)
        mine = mine.reshape(span, 3 * width)

    with jax.named_scope("stale"):
        stale_own = pl.pallas_call(
            select,
            out_shape=jax.ShapeDtypeStruct((span, 2 * width), jnp.bfloat16),
            in_specs=[whole_smem] * 2 + [whole_vmem] * 2,
            out_specs=whole_vmem,
            compiler_params=small_kernel,
            name="pick_stale",
        )(patch_lengths, stale_step, stale_key, stale_value)
        stale = from_neighbours(stale_own)

    mine, stale = lax.optimization_barrier((mine, stale))

    with jax.named_scope("gather_queries"):
        queries = jnp.broadcast_to(mine[None, :, :width], (4, span, width))
        queries = lax.all_to_all(queries, quad, split_axis=0, concat_axis=0, tiled=True)
        queries = queries.reshape(4 * span, width)

    with jax.named_scope("neighbour_keys"):
        fresh = from_neighbours(mine[:, width:])

    with jax.named_scope("attend"):
        parts = pl.pallas_call(
            functools.partial(attend, place=place),
            out_shape=jax.ShapeDtypeStruct((128, 5, 2, width), jnp.bfloat16),
            in_specs=[whole_smem] + [whole_vmem] * 3,
            out_specs=whole_vmem,
            scratch_shapes=[pltpu.VMEM((4 * span, 2 * width), jnp.bfloat16)],
            compiler_params=pltpu.CompilerParams(vmem_limit_bytes=24 << 20),
            cost_estimate=pl.CostEstimate(flops=2 * 2 * 512 * 4096 * 128, bytes_accessed=4 << 20, transcendentals=1 << 20),
            name="attend",
        )(patch_lengths, queries, fresh, stale)

    with jax.named_scope("heads_to_tokens"):
        parts = lax.all_to_all(parts, (quad,) + head, split_axis=0, concat_axis=0, tiled=True)
        return pl.pallas_call(
            combine,
            out_shape=jax.ShapeDtypeStruct((8, 32 * width), jnp.bfloat16),
            in_specs=[whole_vmem],
            out_specs=whole_vmem,
            compiler_params=small_kernel,
            name="combine",
        )(parts.reshape(1280, width))


def solution(mesh):
    fine = Mesh(mesh.devices.reshape(4, 2, 2, 8, 4), (quad, pair, core) + head)
    rows = P(everywhere, None)
    cache = P(None, pipe, head)
    return jax.shard_map(
        on_device,
        mesh=fine,
        in_specs=(rows, rows, rows, cache, cache, P(), P()),
        out_specs=rows,
        check_vma=False,
    )
```
